256 devices in a mesh: bin: 32 (over y, x, core), gcol: 8 (over z).
Axes of the slice: x: 4, y: 4, z: 8, core: 2. Of those that a mesh axis runs over, the one named last changes fastest.
Arguments:
- pair_rows: bfloat16 [16384, 2, 4096], P('bin', None, 'gcol'), may hold values from -5 to 5
- pair_owner: int32 [16384, 1], P('bin'), may hold values from 0 to 31; in each aligned block of 512 rows (0 to 511, 512 to 1023, ...) at most 32 rows name the same one
- pair_offset: int32 [16384], P('bin'), may hold values from 0 to 7
- pair_frac: float32 [16384], P('bin'), may hold values from 0 to 1
Outputs:
- chi_zero: float32 [256, 2, 128, 4096], P('bin', None, None, 'gcol')
The draws below stay inside these ranges and needn't reach their ends.
Inputs may be any that keep to these rules, and one draw needn't show every extreme that they name: `pair_owner`: among the rows of one device at most 32 pairs name the same owner, and in every draw some owner is named by exactly 32 rows of some device.
All inputs are finite; a program needn't handle non-finite values.
Results may differ from the reference program's by a relative error of at most 0.0039.
Values may be sent and summed in bfloat16 or wider, within the bound.
No kernel may reach another device: no remote copies, remote signals or barrier semaphores. Data moves between devices by JAX's collectives and lax.ppermute only.
A program may use at most 64 MiB of HBM per device.

```python
import math
import jax
import jax.numpy as jnp
import numpy as np
from jax import lax

NG = 4096
NB = 256
GW = 128
PAIR_DEV = 512
PAIRS = 16384
NB_DEV = 8
CAP = 32
N_BIN = 32


def place_ends(array, stream_key, least, high):
    shape = array.shape
    index_at = [jax.random.randint(jax.random.fold_in(stream_key, axis), (), 0, shape[axis]) for axis in range(len(shape))]
    array = array.at[tuple(index_at)].set(least)
    longest = shape.index(max(shape))
    index_at[longest] = (index_at[longest] + 1) % shape[longest]
    return array.at[tuple(index_at)].set(high)


def steps_of(rng, dims, cuts, least, high):
    def one(axis_at, blocks):
        heights = jax.random.uniform(jax.random.fold_in(jax.random.fold_in(rng, 6), axis_at), (blocks,), jnp.float32, least / len(cuts), high / len(cuts))
        return jnp.repeat(jnp.exp(heights), dims[axis_at] // blocks).reshape((-1,) + (1,) * (len(dims) - axis_at - 1))

    loudness = one(*cuts[0])
    for cut in cuts[1:]:
        loudness = loudness * one(*cut)
    return loudness


def shared_out(own_key, own, number, rows, amount, top, bound, lean):
    ranking = jax.random.permutation(own_key, amount)
    heavy_load, common = shares(amount, rows * top, bound, lean, True), shares(amount, rows * top, bound, lean, False)
    places = jnp.arange(amount)

    def named(tallies, turn):
        used = int((tallies > 0).sum())
        fixed = max(1, used // 4)
        passed = fixed + (places - fixed + turn * (used - fixed)) % max(1, amount - fixed)
        return jnp.zeros((amount,), jnp.int32).at[ranking[jnp.where(places < fixed, places, passed)]].set(jnp.asarray(tallies, jnp.int32))

    tallies = jnp.where(number % 4 == 0, named(heavy_load, number // 4), named(common, number - number // 4 - 1))
    mixed = jax.random.permutation(jax.random.fold_in(own, 3), amount)
    giver, sink = mixed[0:amount // 2 * 2:2], mixed[1:amount // 2 * 2:2]
    slack = jnp.minimum(tallies[giver] - 1, bound - tallies[sink]) // 2
    slack = jnp.where((giver == ranking[0]) | (sink == ranking[0]) | (tallies[sink] == 0), 0, jnp.maximum(slack, 0))
    passed = jax.random.randint(jax.random.fold_in(own, 4), (amount // 2,), 0, 1 << 20) % (slack + 1)
    tallies = tallies.at[giver].add(-passed).at[sink].add(passed)
    members = jnp.searchsorted(jnp.cumsum(tallies), jnp.arange(rows * top), side="right").astype(jnp.int32)
    table = members.reshape(top, rows).T
    table = table[jax.random.permutation(jax.random.fold_in(own, 1), rows)]
    turn = jax.random.randint(jax.random.fold_in(own, 2), (rows, 1), 0, top)
    return jnp.take_along_axis(table, (jnp.arange(top)[None, :] + turn) % top, axis=1)


def shares(count, total, reach, slope, full):
    weights = [(1 << 20) // math.isqrt(rank ** slope) + 1 for rank in range(1, count + 1)]
    largest = reach if full else min(reach, max(-(-total // count), total * weights[0] // sum(weights)))
    least = 1 if total - largest >= count - 1 else 0
    given, spare = [largest] + [least] * (count - 1), total - largest - least * (count - 1)
    while spare > 0:
        movable = [i for i in range(1, count) if given[i] < largest] or [i for i in range(1, count) if given[i] < reach]
        pool, left = sum([weights[i] for i in movable]), spare
        for i in movable:
            more = min(reach - given[i], max(1, left * weights[i] // pool), spare)
            given[i] = given[i] + more
            spare = spare - more
    return np.array(given)


def noise(stream_key, dims, scale, reach, cuts=(), kind=jnp.bfloat16):
    entries = scale * jax.random.normal(stream_key, dims, jnp.float32)
    if cuts:
        entries = entries * steps_of(stream_key, dims, cuts, -0.22, 0.18)
    return jnp.clip(entries, -reach, reach).astype(kind)


def setup_inputs(seed: int = 0) -> dict:
    key_of = jax.random.split(jax.random.key(seed), 5)
    pair_rows = noise(key_of[0], (PAIRS, 2, NG), 0.35, 5.0, ((0, 32), (2, 8)))
    pair_owner_keys = jax.random.split(jax.random.fold_in(key_of[1], 1), PAIRS // PAIR_DEV)
    pair_owner_turns = jax.random.permutation(jax.random.fold_in(key_of[1], 3), PAIRS // PAIR_DEV)
    pair_owner = jax.vmap(lambda own, number: shared_out(jax.random.fold_in(key_of[1], 2), own, number, PAIR_DEV, N_BIN, 1, CAP, 2))(pair_owner_keys, pair_owner_turns).reshape((PAIRS, 1))
    pair_offset = place_ends(jax.random.randint(key_of[2], (PAIRS,), 0, NB_DEV), jax.random.fold_in(key_of[2], 1), 0, NB_DEV - 1).astype(jnp.int32)
    pair_frac = jnp.clip(1.0 * jax.random.uniform(key_of[3], (PAIRS,), jnp.float32) ** steps_of(key_of[3], (PAIRS,), ((0, 32),), -0.2, 0.2), 0.0, 1.0)
    return {"pair_rows": pair_rows, "pair_owner": pair_owner, "pair_offset": pair_offset, "pair_frac": pair_frac}


def hilbert_table(bin_total):
    column = jnp.arange(bin_total, dtype=jnp.float32)
    difference = column[:, None] - column[None, :]
    second = column[:, None] + column[None, :] + 1.0
    real_part = difference / (difference * difference + 1.0) - second / (second * second + 1.0)
    imag_part = 1.0 / (second * second + 1.0) - 1.0 / (difference * difference + 1.0)
    return real_part, imag_part


def apply_hilbert(spectral):
    bin_total = spectral.shape[0]
    real_table, imag_table = hilbert_table(bin_total)
    flat_real = spectral[:, 0].astype(jnp.float32).reshape(bin_total, -1)
    flat_imag = spectral[:, 1].astype(jnp.float32).reshape(bin_total, -1)
    highest = lax.Precision.HIGHEST
    out_real = jnp.dot(real_table, flat_real, precision=highest) - jnp.dot(imag_table, flat_imag, precision=highest)
    out_imag = jnp.dot(real_table, flat_imag, precision=highest) + jnp.dot(imag_table, flat_real, precision=highest)
    return jnp.stack([out_real, out_imag], axis=1).reshape(spectral.shape)


def weight_table(pair_offset, pair_frac, bin_count):
    lower_weight = (1.0 - pair_frac).astype(jnp.bfloat16)
    upper_weight = pair_frac.astype(jnp.bfloat16)
    column = jnp.arange(bin_count, dtype=jnp.int32)
    nothing = jnp.zeros((), jnp.bfloat16)
    lower_part = jnp.where(column[None, :] == pair_offset[:, None], lower_weight[:, None], nothing)
    upper_part = jnp.where(column[None, :] == pair_offset[:, None] + 1, upper_weight[:, None], nothing)
    return lower_part + upper_part


def spectral_tile(weights, head_vals, row_data):
    scaled = (weights.astype(jnp.float32)[:, None, :, None] * head_vals.astype(jnp.float32)[:, :, None, :]).astype(jnp.bfloat16)
    products = jnp.einsum("rakg,rbc->akgbc", scaled.astype(jnp.float32), row_data.astype(jnp.float32))
    real_part = products[0, :, :, 0] + products[1, :, :, 1]
    imag_part = products[0, :, :, 1] - products[1, :, :, 0]
    return jnp.stack([real_part, imag_part], axis=1)


def reference(pair_rows, pair_owner, pair_offset, pair_frac):
    owners = pair_owner[:, 0].astype(jnp.int32)
    weights = weight_table(pair_offset, pair_frac, NB_DEV + 1)
    head_vals = pair_rows[:, :, :GW]
    ordering = jnp.argsort(owners, stable=True).astype(jnp.int32)
    counts = jnp.sum((owners[:, None] == jnp.arange(N_BIN, dtype=jnp.int32)[None, :]).astype(jnp.int32), axis=0).astype(jnp.int32)
    starts = (jnp.cumsum(counts) - counts).astype(jnp.int32)
    window_rows = 2 * PAIR_DEV

    def padded(values):
        filler = jnp.zeros((window_rows,) + values.shape[1:], values.dtype)
        return jnp.concatenate([values[ordering], filler], axis=0)

    sorted_rows = padded(pair_rows)
    sorted_weights = padded(weights)
    sorted_head = padded(head_vals)

    def one_owner(target):
        first_row = starts[target]
        is_alive = jnp.arange(window_rows, dtype=jnp.int32) < counts[target]

        def cut_rows(values):
            return lax.dynamic_slice_in_dim(values, first_row, window_rows, 0)

        weights_here = jnp.where(is_alive[:, None], cut_rows(sorted_weights), jnp.zeros((), jnp.bfloat16))
        return spectral_tile(weights_here, cut_rows(sorted_head), cut_rows(sorted_rows))

    bin_tiles = lax.map(one_owner, jnp.arange(N_BIN, dtype=jnp.int32))
    upper_tiles = bin_tiles[:, NB_DEV]
    previous = jnp.concatenate([jnp.zeros_like(upper_tiles[:1]), upper_tiles[:-1]], axis=0)
    lower_tiles = bin_tiles[:, :NB_DEV].at[:, 0].add(previous)
    spectral = lower_tiles.reshape(NB, 2, GW, NG).astype(jnp.bfloat16)
    return apply_hilbert(spectral)
```

```python
import functools

import jax
import jax.numpy as jnp
from jax import lax
from jax.experimental import pallas as pl
from jax.experimental.pallas import tpu as pltpu
from jax.sharding import PartitionSpec as P

NB = 256
GW = 128
BF16 = jnp.bfloat16
F32 = jnp.float32
VMEM_BYTES = 48 * 1024 * 1024
PARTS = 2


def dot(a, b):
    return jnp.dot(a, b, preferred_element_type=F32)


def iota(shape, axis):
    return lax.broadcasted_iota(jnp.int32, shape, axis)


def call(kernel, out_shape, **options):
    return pl.pallas_call(
        kernel,
        out_shape=out_shape,
        compiler_params=pltpu.CompilerParams(vmem_limit_bytes=VMEM_BYTES),
        **options,
    )


def slot_onehot(target, slot_count):
    pairs = target.shape[1]
    return (iota((slot_count, pairs), 0) == target).astype(F32).astype(BF16)


def pack_rows_kernel(owner_ref, rows_ref, target_ref, *out_refs):
    groups, _, capacity, width = out_refs[0].shape
    pairs = owner_ref.shape[1]
    owner = owner_ref[...]
    named = (iota((groups, pairs), 0) == owner).astype(F32)
    before = (iota((pairs, pairs), 0) < iota((pairs, pairs), 1)).astype(F32).astype(BF16)
    rank = jnp.sum(dot(named.astype(BF16), before) * named, axis=0, keepdims=True)
    target = owner * capacity + rank.astype(jnp.int32)
    target_ref[...] = target
    onehot = slot_onehot(target, groups * capacity)
    for part, out_ref in enumerate(out_refs):
        for c in range(2):
            values = rows_ref[c, :, part * width : (part + 1) * width]
            packed = dot(onehot, values).astype(BF16)
            out_ref[:, c] = packed.reshape(groups, capacity, width)


def pack_heads_kernel(target_ref, head_ref, weight_ref, out_ref):
    groups, capacity, width = out_ref.shape
    onehot = slot_onehot(target_ref[...], groups * capacity)
    head = dot(onehot, head_ref[...]).astype(BF16)
    weight = dot(onehot, weight_ref[...]).astype(BF16)
    split = head_ref.shape[1]
    out_ref[:, :, :split] = head.reshape(groups, capacity, split)
    out_ref[:, :, split:] = weight.reshape(groups, capacity, width - split)


def turn_kernel(in_ref, head_ref, weight_ref):
    groups, capacity, width = in_ref.shape
    turned = in_ref[...].reshape(groups * capacity, width).astype(F32).T
    head_ref[...] = turned[: 2 * GW].astype(BF16)
    weight_ref[...] = turned[2 * GW : 2 * GW + weight_ref.shape[0]]


def row_parts(rows_ref):
    groups, _, capacity, width = rows_ref.shape
    return [rows_ref[:, c].reshape(groups * capacity, width) for c in range(2)]


def complex_dot(left, right):
    real = dot(left[0], right[0]) + dot(left[1], right[1])
    imag = dot(left[0], right[1]) - dot(left[1], right[0])
    return real, imag


def upper_kernel(own_bins, head_ref, weight_ref, rows_ref, out_ref):
    weight = weight_ref[own_bins : own_bins + 1]
    scaled = [
        (head_ref[c * GW : (c + 1) * GW].astype(F32) * weight).astype(BF16) for c in range(2)
    ]
    real, imag = complex_dot(scaled, row_parts(rows_ref))
    out_ref[0] = real
    out_ref[1] = imag


def spectral_kernel(own_bins, head_ref, weight_ref, rows_ref, upper_ref, out_ref):
    chunk, per, _, width = out_ref.shape
    window = chunk * per
    slots = weight_ref.shape[1]
    at = pl.program_id(0) * window
    weight = weight_ref[:own_bins]
    scaled = []
    for c in range(2):
        head = head_ref[pl.ds(pl.multiple_of(c * GW + at, window), window)].astype(F32)
        scaled.append(
            (head[:, None, :] * weight[None]).astype(BF16).reshape(window * own_bins, slots)
        )
    result = complex_dot(scaled, row_parts(rows_ref))
    lowest = iota((window, own_bins, width), 1) == 0
    held = []
    for c in range(2):
        extra = upper_ref[c].reshape(window, 1, width)
        held.append(
            result[c].reshape(window, own_bins, width) + jnp.where(lowest, extra, 0.0)
        )
    out_ref[...] = (
        jnp.concatenate(held, axis=1).astype(BF16).reshape(chunk, per, 2 * own_bins, width)
    )


def hilbert_kernel(high_ref, low_ref, in_ref, out_ref):
    groups, per, depth, width = in_ref.shape
    for g in range(per):
        values = in_ref[:, g].reshape(groups * depth, width)
        result = dot(high_ref[...], values) + dot(low_ref[...], values)
        out_ref[:, g] = result.astype(BF16).reshape(groups, depth, width)


def final_kernel(in_ref, *refs):
    out_ref, wide = refs[-2:]
    step = pl.program_id(0)
    own_bins = pl.num_programs(0)
    rows = in_ref.shape[0] * in_ref.shape[1]
    depth, width = in_ref.shape[2:]

    @pl.when(step == 0)
    def _():
        values = in_ref[...].astype(F32).reshape(rows * depth, width)
        for k in range(width // 128):
            wide[k] = values[:, k * 128 : (k + 1) * 128]

    for c in range(2):
        for k in range(width // 128):
            out_ref[0, c, :, k * 128 : (k + 1) * 128] = wide[
                k, pl.ds(c * (depth // 2) + step, rows, stride=depth), :
            ]


def hilbert_table(bin_total):
    column = jnp.arange(bin_total, dtype=F32)
    difference = column[:, None] - column[None, :]
    second = column[:, None] + column[None, :] + 1.0
    real_part = difference / (difference * difference + 1.0) - second / (second * second + 1.0)
    imag_part = 1.0 / (second * second + 1.0) - 1.0 / (difference * difference + 1.0)
    return (real_part, imag_part)


def split_table(groups, own_bins):
    real, imag = (
        part.reshape(groups, own_bins, groups, own_bins) for part in hilbert_table(NB)
    )
    upper = jnp.stack([real, -imag], axis=3)
    lower = jnp.stack([imag, real], axis=3)
    table = jnp.stack([upper, lower], axis=1).reshape(2 * NB, 2 * NB)
    high = table.astype(BF16)
    low = (table - high.astype(F32)).astype(BF16)
    return high, low


def weight_table(pair_offset, pair_frac, bin_count):
    lower_weight = (1.0 - pair_frac).astype(BF16)
    upper_weight = pair_frac.astype(BF16)
    column = jnp.arange(bin_count, dtype=jnp.int32)
    nothing = jnp.zeros((), BF16)
    lower_part = jnp.where(column[None, :] == pair_offset[:, None], lower_weight[:, None], nothing)
    upper_part = jnp.where(
        column[None, :] == pair_offset[:, None] + 1, upper_weight[:, None], nothing
    )
    return lower_part + upper_part


def from_first(block, axis):
    place = lax.axis_index(axis)
    ahead = lax.ppermute(block, axis, [(0, 3)])
    behind = lax.ppermute(block, axis, [(0, 5)])
    block = jnp.where(place == 3, ahead, jnp.where(place == 5, behind, block))
    ahead = lax.ppermute(block, axis, [(0, 1), (3, 4), (5, 6)])
    behind = lax.ppermute(block, axis, [(0, 7), (3, 2)])
    use_ahead = (place == 1) | (place == 4) | (place == 6)
    use_behind = (place == 7) | (place == 2)
    return jnp.where(use_ahead, ahead, jnp.where(use_behind, behind, block))


def exchange(block):
    return lax.all_to_all(block, "bin", split_axis=0, concat_axis=0, tiled=True)


def on_device(pair_rows, pair_owner, pair_offset, pair_frac):
    groups = lax.axis_size("bin")
    pairs, _, columns = pair_rows.shape
    capacity = 2 * pairs // groups
    slots = groups * capacity
    own_bins = NB // groups
    per = GW // groups
    width = columns // PARTS
    blocks = 4
    shape = jax.ShapeDtypeStruct

    by_part = jnp.swapaxes(pair_rows, 0, 1)
    head = from_first(
        jnp.swapaxes(by_part[:, :, :GW], 0, 1).reshape(pairs, 2 * GW), "gcol"
    )
    target, *packed = call(
        pack_rows_kernel,
        [shape((1, pairs), jnp.int32)]
        + [shape((groups, 2, capacity, width), BF16)] * PARTS,
    )(pair_owner.reshape(1, pairs), by_part)
    weights = weight_table(pair_offset, pair_frac, 128)
    packed_heads = call(pack_heads_kernel, shape((groups, capacity, 2 * GW + 128), BF16))(
        target, head, weights
    )
    got_rows = [None] * PARTS
    got_rows[0] = exchange(packed[0])
    got_heads = exchange(packed_heads)
    for part in range(1, PARTS):
        got_rows[part] = exchange(packed[part])
    high, low = split_table(groups, own_bins)

    turned, got_weights = call(
        turn_kernel, [shape((2 * GW, slots), BF16), shape((16, slots), F32)]
    )(got_heads)

    route = [(i, i + 1) for i in range(groups - 1)]
    whole = lambda *dims: pl.BlockSpec(dims, lambda i: (0,) * len(dims))
    spectral = []
    for part in range(PARTS):
        upper = call(
            functools.partial(upper_kernel, own_bins), shape((2, GW, width), F32)
        )(turned, got_weights, got_rows[part])
        upper = lax.ppermute(upper, "bin", route)
        spectral.append(
            call(
                functools.partial(spectral_kernel, own_bins),
                shape((groups, per, 2 * own_bins, width), BF16),
                grid=(blocks,),
                in_specs=[
                    whole(2 * GW, slots),
                    whole(16, slots),
                    whole(groups, 2, capacity, width),
                    pl.BlockSpec((2, GW // blocks, width), lambda i: (0, i, 0)),
                ],
                out_specs=pl.BlockSpec(
                    (groups // blocks, per, 2 * own_bins, width), lambda i: (i, 0, 0, 0)
                ),
            )(turned, got_weights, got_rows[part], upper)
        )
    spectral = [exchange(block) for block in spectral]
    chi = [
        exchange(call(hilbert_kernel, shape(block.shape, BF16))(high, low, block))
        for block in spectral
    ]
    out = None
    for part in range(PARTS):
        earlier = [] if out is None else [out]
        out = call(
            final_kernel,
            shape((own_bins, 2, GW, columns), F32),
            grid=(own_bins,),
            in_specs=[whole(groups, per, 2 * own_bins, width)]
            + [pl.BlockSpec(memory_space=pl.ANY)] * len(earlier),
            out_specs=pl.BlockSpec((1, 2, GW, width), lambda i, part=part: (i, 0, 0, part)),
            scratch_shapes=[pltpu.VMEM((width // 128, GW * 2 * own_bins, 128), F32)],
            input_output_aliases={1: 0} if earlier else {},
        )(chi[part], *earlier)
    return out


def solution(mesh):
    placed = (P("bin", None, "gcol"), P("bin", None), P("bin"), P("bin"))
    return jax.shard_map(
        on_device,
        mesh=mesh,
        in_specs=placed,
        out_specs=P("bin", None, None, "gcol"),
        check_vma=False,
    )
```

```python
import functools

import jax
import jax.numpy as jnp
from jax import lax
from jax.experimental import pallas as pl
from jax.experimental.pallas import tpu as pltpu
from jax.sharding import PartitionSpec as P

NB = 256
GW = 128
BF16 = jnp.bfloat16
F32 = jnp.float32
VMEM_BYTES = 24 * 1024 * 1024


def dot(a, b):
    return jnp.dot(a, b, preferred_element_type=F32)


def iota(shape, axis):
    return lax.broadcasted_iota(jnp.int32, shape, axis)


def call(kernel, out_shape, **options):
    return pl.pallas_call(
        kernel,
        out_shape=out_shape,
        compiler_params=pltpu.CompilerParams(vmem_limit_bytes=VMEM_BYTES),
        **options,
    )


def pack_kernel(quarter_ref, owner_ref, offset_ref, frac_ref, rows_ref, first_ref, rest_ref):
    groups, _, capacity, _ = rest_ref.shape
    lanes = first_ref.shape[2]
    extra = first_ref.shape[1] - 2 * capacity
    pairs = owner_ref.shape[1]
    owner = owner_ref[...]
    named = (iota((groups, pairs), 0) == owner).astype(F32)
    before = (iota((pairs, pairs), 0) < iota((pairs, pairs), 1)).astype(F32).astype(BF16)
    rank = jnp.sum(dot(named.astype(BF16), before) * named, axis=0, keepdims=True)
    target = owner * capacity + rank.astype(jnp.int32)
    onehot = (iota((groups * capacity, pairs), 0) == target).astype(F32).astype(BF16)
    for c in range(2):
        packed = dot(onehot, rows_ref[c]).astype(BF16).reshape(groups, capacity, -1)
        first_ref[:, c * capacity : (c + 1) * capacity] = packed[:, :, :lanes]
        rest_ref[:, c] = packed[:, :, lanes:]

    frac = frac_ref[...]
    place = iota((extra, pairs), 0)
    weight = jnp.where(place == offset_ref[...], (1.0 - frac).astype(BF16).astype(F32), 0.0)
    weight += jnp.where(place == offset_ref[...] + 1, frac.astype(BF16).astype(F32), 0.0)
    weight = lax.dot_general(
        weight.astype(BF16), onehot, (((1,), (1,)), ((), ())), preferred_element_type=F32
    )
    share = lanes // capacity
    quarter = quarter_ref[0]
    mine = iota((extra, lanes), 1) // capacity == quarter
    for group in range(groups):
        tile = weight[:, group // share * lanes : (group // share + 1) * lanes]
        turn = (quarter + share - group % share) % share * capacity
        tile = jnp.where(mine, pltpu.roll(tile, turn, 1), 0.0)
        first_ref[group, 2 * capacity :] = tile.astype(BF16)


def turn_kernel(own_bins, use_ref, got_ref, *refs):
    heads = refs[:3]
    head_ref, weight_ref, high_ref, low_ref = refs[3:]
    groups, double, lanes = heads[0].shape
    capacity = double // 2
    share = lanes // capacity
    for choice, source in enumerate(heads):

        @pl.when(use_ref[0] == choice)
        def _(source=source):
            for c in range(2):
                part = source[:, c * capacity : (c + 1) * capacity]
                part = part.reshape(groups * capacity, lanes).astype(F32)
                head_ref[c * lanes : (c + 1) * lanes] = part.T.astype(BF16)

    for at in range(groups // share):
        tile = got_ref[share * at, double:].astype(F32)
        for k in range(1, share):
            tile += got_ref[share * at + k, double:].astype(F32)
        weight_ref[:, at * lanes : (at + 1) * lanes] = tile
    table_kernel(own_bins, high_ref, low_ref)


def complex_dot(left, right):
    real = dot(left[0], right[0]) + dot(left[1], right[1])
    imag = dot(left[0], right[1]) - dot(left[1], right[0])
    return real, imag


def spectral_kernel(own_bins, head_ref, weight_ref, first_ref, rest_ref, out_ref, rows):
    groups, _, capacity, _ = rest_ref.shape
    lanes = first_ref.shape[2]
    chunk, depth, width = out_ref.shape
    bins = 2 * own_bins
    per = depth // (bins + 2)
    window = chunk * per
    slots = weight_ref.shape[1]
    at = pl.program_id(0) * window

    @pl.when(pl.program_id(0) == 0)
    def _():
        for c in range(2):
            first = first_ref[:, c * capacity : (c + 1) * capacity]
            rows[c, :, :lanes] = first.reshape(groups * capacity, lanes)
            rows[c, :, lanes:] = rest_ref[:, c].reshape(groups * capacity, -1)

    lower, upper = [], []
    for c in range(2):
        head = head_ref[pl.ds(pl.multiple_of(c * GW + at, window), window)].astype(F32)
        scaled = (head[:, None, :] * weight_ref[:own_bins][None]).astype(BF16)
        lower.append(scaled.reshape(window * own_bins, slots))
        upper.append((head * weight_ref[own_bins : own_bins + 1]).astype(BF16))
    result = [part.reshape(window, own_bins, width) for part in complex_dot(lower, rows)]
    result = jnp.concatenate(result, axis=1).reshape(chunk, per * bins, width)
    extra = [part.reshape(chunk, per, width) for part in complex_dot(upper, rows)]
    out_ref[...] = jnp.concatenate([result] + extra, axis=1).astype(BF16)


def hilbert_kernel(own_bins, high_ref, low_ref, in_ref, out_ref):
    groups, per, bins, width = out_ref.shape
    extra = in_ref[: groups - 1, per * bins :].astype(F32)
    place = iota((groups, bins, width), 1)
    for g in range(per):
        values = in_ref[:, g * bins : (g + 1) * bins].astype(F32)
        for c in range(2):
            at = c * per + g
            behind = jnp.concatenate(
                [jnp.zeros((1, 1, width), F32), extra[:, at : at + 1]], axis=0
            )
            values = values + jnp.where(place == c * own_bins, behind, 0.0)
        values = values.astype(BF16).reshape(groups * bins, width)
        result = dot(high_ref[...], values) + dot(low_ref[...], values)
        out_ref[:, g] = result.astype(BF16).reshape(groups, bins, width)


def final_kernel(in_ref, *refs):
    out_ref, wide = refs[-2:]
    step = pl.program_id(0)
    own_bins = pl.num_programs(0)
    rows = in_ref.shape[0] * in_ref.shape[1]
    depth, width = in_ref.shape[2:]

    @pl.when(step == 0)
    def _():
        values = in_ref[...].astype(F32).reshape(rows * depth, width)
        for k in range(width // 128):
            wide[k] = values[:, k * 128 : (k + 1) * 128]

    for c in range(2):
        for k in range(width // 128):
            out_ref[0, c, :, k * 128 : (k + 1) * 128] = wide[
                k, pl.ds(c * (depth // 2) + step, rows, stride=depth), :
            ]


def table_kernel(own_bins, high_ref, low_ref):
    shape = high_ref.shape
    row = iota(shape, 0)
    column = iota(shape, 1)
    group = 2 * own_bins
    frequency = (row // group * own_bins + row % own_bins).astype(F32)
    bin_at = (column // group * own_bins + column % own_bins).astype(F32)
    row_imag = row // own_bins % 2 == 1
    column_imag = column // own_bins % 2 == 1
    difference = frequency - bin_at
    second = frequency + bin_at + 1.0
    first_scale = 1.0 / (difference * difference + 1.0)
    second_scale = 1.0 / (second * second + 1.0)
    real_part = difference * first_scale - second * second_scale
    imag_part = second_scale - first_scale
    crossed = jnp.where(row_imag, imag_part, -imag_part)
    table = jnp.where(row_imag == column_imag, real_part, crossed)
    high = table.astype(BF16)
    high_ref[...] = high
    low_ref[...] = (table - high.astype(F32)).astype(BF16)


def from_first(block, axis):
    place = lax.axis_index(axis)
    ahead = lax.ppermute(block, axis, [(0, 3)])
    behind = lax.ppermute(block, axis, [(0, 5)])
    block = jnp.where(place == 3, ahead, jnp.where(place == 5, behind, block))
    ahead = lax.ppermute(block, axis, [(0, 1), (3, 4), (5, 6)])
    behind = lax.ppermute(block, axis, [(0, 7), (3, 2)])
    use_ahead = (place == 1) | (place == 4) | (place == 6)
    use_behind = (place == 7) | (place == 2)
    use = jnp.where(use_ahead, 1, jnp.where(use_behind, 2, 0))
    return use.reshape(1), (block, ahead, behind)


def exchange(block):
    return lax.all_to_all(block, "bin", split_axis=0, concat_axis=0, tiled=True)


def on_device(pair_rows, pair_owner, pair_offset, pair_frac):
    groups = lax.axis_size("bin")
    pairs, _, columns = pair_rows.shape
    capacity = 2 * pairs // groups
    slots = groups * capacity
    own_bins = NB // groups
    per = GW // groups
    blocks = 4
    shape = jax.ShapeDtypeStruct
    scalar = pl.BlockSpec(memory_space=pltpu.SMEM)
    here = pl.BlockSpec(memory_space=pltpu.VMEM)

    quarter = lax.axis_index("bin") % (GW // capacity)
    first, rest = call(
        pack_kernel,
        [
            shape((groups, 2 * capacity + 16, GW), BF16),
            shape((groups, 2, capacity, columns - GW), BF16),
        ],
        in_specs=[scalar] + [here] * 4,
    )(
        quarter.reshape(1),
        pair_owner.reshape(1, pairs),
        pair_offset.reshape(1, pairs),
        pair_frac.reshape(1, pairs),
        jnp.swapaxes(pair_rows, 0, 1),
    )
    first = exchange(first)
    rest = exchange(rest)
    use, heads = from_first(first[:, : 2 * capacity], "gcol")
    head, weight, high, low = call(
        functools.partial(turn_kernel, own_bins),
        [
            shape((2 * GW, slots), BF16),
            shape((16, slots), F32),
            shape((2 * NB, 2 * NB), BF16),
            shape((2 * NB, 2 * NB), BF16),
        ],
        in_specs=[scalar] + [here] * 4,
    )(use, first, *heads)

    whole = lambda *dims: pl.BlockSpec(dims, lambda i: (0,) * len(dims))
    depth = per * (2 * own_bins + 2)
    spectral = call(
        functools.partial(spectral_kernel, own_bins),
        shape((groups, depth, columns), BF16),
        grid=(blocks,),
        in_specs=[
            whole(2 * GW, slots),
            whole(16, slots),
            whole(*first.shape),
            whole(*rest.shape),
        ],
        out_specs=pl.BlockSpec((groups // blocks, depth, columns), lambda i: (i, 0, 0)),
        scratch_shapes=[pltpu.VMEM((2, slots, columns), BF16)],
    )(head, weight, first, rest)
    chi = call(
        functools.partial(hilbert_kernel, own_bins),
        shape((groups, per, 2 * own_bins, columns), BF16),
    )(high, low, exchange(spectral))
    chi = exchange(chi)
    return call(
        final_kernel,
        shape((own_bins, 2, GW, columns), F32),
        grid=(own_bins,),
        in_specs=[whole(groups, per, 2 * own_bins, columns)],
        out_specs=pl.BlockSpec((1, 2, GW, columns), lambda i: (i, 0, 0, 0)),
        scratch_shapes=[pltpu.VMEM((columns // 128, GW * 2 * own_bins, 128), F32)],
    )(chi)


def solution(mesh):
    placed = (P("bin", None, "gcol"), P("bin", None), P("bin"), P("bin"))
    return jax.shard_map(
        on_device,
        mesh=mesh,
        in_specs=placed,
        out_specs=P("bin", None, None, "gcol"),
        check_vma=False,
    )
```

```python
import functools

import jax
import jax.numpy as jnp
from jax import lax
from jax.experimental import pallas as pl
from jax.experimental.pallas import tpu as pltpu
from jax.sharding import PartitionSpec as P

NB = 256
GW = 128
LANES = 128
EXTRA = 16
BF16 = jnp.bfloat16
F32 = jnp.float32
VMEM_BYTES = 24 * 1024 * 1024


def dot(a, b):
    return jnp.dot(a, b, preferred_element_type=F32)


def iota(shape, axis):
    return lax.broadcasted_iota(jnp.int32, shape, axis)


def call(kernel, out_shape, **options):
    return pl.pallas_call(
        kernel,
        out_shape=out_shape,
        compiler_params=pltpu.CompilerParams(vmem_limit_bytes=VMEM_BYTES),
        **options,
    )


def slot_onehot(target, slots):
    return (iota((slots, target.shape[1]), 0) == target).astype(F32).astype(BF16)


def tile_rows(tile, part, capacity):
    at = (2 * tile + part) * capacity
    return slice(at, at + capacity)


def pack_rows_kernel(
    quarter_ref, owner_ref, offset_ref, frac_ref, rows_ref, head_ref, target_ref, copy_ref, out_ref
):
    groups, depth, _ = out_ref.shape
    pairs = owner_ref.shape[1]
    tiles = rows_ref.shape[2] // LANES
    capacity = (depth - EXTRA) // (2 * tiles)
    copy_ref[...] = head_ref[...]
    owner = owner_ref[...]
    named = (iota((groups, pairs), 0) == owner).astype(F32)
    before = (iota((pairs, pairs), 0) < iota((pairs, pairs), 1)).astype(F32).astype(BF16)
    rank = jnp.sum(dot(named.astype(BF16), before) * named, axis=0, keepdims=True)
    target = owner * capacity + rank.astype(jnp.int32)
    target_ref[...] = target
    onehot = slot_onehot(target, groups * capacity)
    for c in range(2):
        packed = dot(onehot, rows_ref[c]).astype(BF16)
        for tile in range(tiles):
            part = packed[:, tile * LANES : (tile + 1) * LANES]
            out_ref[:, tile_rows(tile, c, capacity)] = part.reshape(groups, capacity, LANES)

    frac = frac_ref[...]
    place = iota((EXTRA, pairs), 0)
    weight = jnp.where(place == offset_ref[...], (1.0 - frac).astype(BF16).astype(F32), 0.0)
    weight += jnp.where(place == offset_ref[...] + 1, frac.astype(BF16).astype(F32), 0.0)
    weight = lax.dot_general(
        weight.astype(BF16), onehot, (((1,), (1,)), ((), ())), preferred_element_type=F32
    )
    share = LANES // capacity
    quarter = quarter_ref[0]
    mine = iota((EXTRA, LANES), 1) // capacity == quarter
    for group in range(groups):
        tile = weight[:, group // share * LANES : (group // share + 1) * LANES]
        turn = (quarter + share - group % share) % share * capacity
        tile = jnp.where(mine, pltpu.roll(tile, turn, 1), 0.0)
        out_ref[group, depth - EXTRA :] = tile.astype(BF16)


def pack_heads_kernel(target_ref, head_ref, arrived_ref, out_ref):
    groups, double, lanes = out_ref.shape
    capacity = double // 2
    onehot = slot_onehot(target_ref[...], groups * capacity)
    packed = dot(onehot, head_ref[...]).astype(BF16)
    for c in range(2):
        part = packed[:, c * lanes : (c + 1) * lanes]
        out_ref[:, c * capacity : (c + 1) * capacity] = part.reshape(groups, capacity, lanes)


def prepare_kernel(own_bins, got_ref, got_head_ref, head_ref, weight_ref, rows_ref, upper_ref):
    groups, double, lanes = got_head_ref.shape
    capacity = double // 2
    slots = groups * capacity
    share = LANES // capacity
    extra = got_ref.shape[1] - EXTRA
    for c in range(2):
        for tile in range(rows_ref.shape[2] // LANES):
            part = got_ref[:, tile_rows(tile, c, capacity)].reshape(slots, LANES)
            rows_ref[c, :, tile * LANES : (tile + 1) * LANES] = part
        head = got_head_ref[:, c * capacity : (c + 1) * capacity].reshape(slots, lanes)
        head_ref[c * lanes : (c + 1) * lanes] = head.astype(F32).T.astype(BF16)
    for at in range(groups // share):
        tile = got_ref[share * at, extra:].astype(F32)
        for k in range(1, share):
            tile += got_ref[share * at + k, extra:].astype(F32)
        weight_ref[:, at * LANES : (at + 1) * LANES] = tile
    weight = weight_ref[own_bins : own_bins + 1]
    scaled = [
        (head_ref[c * GW : (c + 1) * GW].astype(F32) * weight).astype(BF16) for c in range(2)
    ]
    for c, part in enumerate(complex_dot(scaled, rows_ref)):
        upper_ref[c] = part.astype(BF16)


def complex_dot(left, right):
    real = dot(left[0], right[0]) + dot(left[1], right[1])
    imag = dot(left[0], right[1]) - dot(left[1], right[0])
    return real, imag


def spectral_kernel(own_bins, head_ref, weight_ref, rows_ref, out_ref):
    chunk, per, bins, width = out_ref.shape
    window = chunk * per
    slots = weight_ref.shape[1]
    at = pl.program_id(0) * window
    scaled = []
    for c in range(2):
        head = head_ref[pl.ds(pl.multiple_of(c * GW + at, window), window)].astype(F32)
        part = (head[:, None, :] * weight_ref[:own_bins][None]).astype(BF16)
        scaled.append(part.reshape(window * own_bins, slots))
    result = [part.reshape(window, own_bins, width) for part in complex_dot(scaled, rows_ref)]
    result = jnp.concatenate(result, axis=1).reshape(chunk, per, bins, width)
    out_ref[...] = result.astype(BF16)


def carry_kernel(spectral_ref, upper_ref, out_ref):
    groups, per, bins, width = out_ref.shape
    place = iota((groups * per, bins, width), 1)
    values = spectral_ref[...].astype(F32).reshape(groups * per, bins, width)
    for c in range(2):
        upper = upper_ref[c].astype(F32).reshape(groups * per, 1, width)
        values = values + jnp.where(place == c * (bins // 2), upper, 0.0)
    out_ref[...] = values.astype(BF16).reshape(groups, per, bins, width)


def table_kernel(own_bins, high_ref, low_ref):
    shape = high_ref.shape
    row = iota(shape, 0)
    column = iota(shape, 1)
    group = 2 * own_bins
    frequency = (row // group * own_bins + row % own_bins).astype(F32)
    bin_at = (column // group * own_bins + column % own_bins).astype(F32)
    row_imag = row // own_bins % 2 == 1
    column_imag = column // own_bins % 2 == 1
    difference = frequency - bin_at
    second = frequency + bin_at + 1.0
    first_scale = 1.0 / (difference * difference + 1.0)
    second_scale = 1.0 / (second * second + 1.0)
    real_part = difference * first_scale - second * second_scale
    imag_part = second_scale - first_scale
    crossed = jnp.where(row_imag, imag_part, -imag_part)
    table = jnp.where(row_imag == column_imag, real_part, crossed)
    high = table.astype(BF16)
    high_ref[...] = high
    low_ref[...] = (table - high.astype(F32)).astype(BF16)


def hilbert_kernel(own_bins, in_ref, out_ref, high, low):
    groups, per, bins, width = out_ref.shape
    table_kernel(own_bins, high, low)
    for g in range(per):
        values = in_ref[:, g].reshape(groups * bins, width)
        result = dot(high[...], values) + dot(low[...], values)
        out_ref[:, g] = result.astype(BF16).reshape(groups, bins, width)


def final_kernel(in_ref, out_ref, wide):
    groups, per, depth, lanes = in_ref.shape
    wide[...] = in_ref[...].astype(F32).reshape(groups * per * depth, lanes)
    for c in range(2):
        for step in range(depth // 2):
            out_ref[step, c] = wide[
                pl.ds(c * (depth // 2) + step, groups * per, stride=depth), :
            ]


def from_first(block, axis):
    place = lax.axis_index(axis)
    ahead = lax.ppermute(block, axis, [(0, 3)])
    behind = lax.ppermute(block, axis, [(0, 5)])
    block = jnp.where(place == 3, ahead, jnp.where(place == 5, behind, block))
    ahead = lax.ppermute(block, axis, [(0, 1), (3, 4), (5, 6)])
    behind = lax.ppermute(block, axis, [(0, 7), (3, 2)])
    use_ahead = (place == 1) | (place == 4) | (place == 6)
    use_behind = (place == 7) | (place == 2)
    return jnp.where(use_ahead, ahead, jnp.where(use_behind, behind, block))


def exchange(block):
    return lax.all_to_all(block, "bin", split_axis=0, concat_axis=0, tiled=True)


def on_device(pair_rows, pair_owner, pair_offset, pair_frac):
    groups = lax.axis_size("bin")
    pairs, _, columns = pair_rows.shape
    capacity = 2 * pairs // groups
    slots = groups * capacity
    own_bins = NB // groups
    per = GW // groups
    blocks = 4
    shape = jax.ShapeDtypeStruct
    scalar = pl.BlockSpec(memory_space=pltpu.SMEM)
    here = pl.BlockSpec(memory_space=pltpu.VMEM)

    quarter = lax.axis_index("bin") % (LANES // capacity)
    by_part = jnp.swapaxes(pair_rows, 0, 1)
    target, head, packed = call(
        pack_rows_kernel,
        [
            shape((1, pairs), jnp.int32),
            shape((pairs, 2 * GW), BF16),
            shape((groups, 2 * capacity * columns // LANES + EXTRA, LANES), BF16),
        ],
        in_specs=[scalar] + [here] * 5,
    )(
        quarter.reshape(1),
        pair_owner.reshape(1, pairs),
        pair_offset.reshape(1, pairs),
        pair_frac.reshape(1, pairs),
        by_part,
        pair_rows[:, :, :GW].reshape(pairs, 2 * GW),
    )
    got = exchange(packed)
    head = from_first(head, "gcol")
    got_head = exchange(
        call(
            pack_heads_kernel,
            shape((groups, 2 * capacity, GW), BF16),
            in_specs=[here] * 2 + [pl.BlockSpec(memory_space=pl.ANY)],
        )(target, head, got)
    )

    whole = lambda *dims: pl.BlockSpec(dims, lambda i: (0,) * len(dims))
    head, weight, rows, upper = call(
        functools.partial(prepare_kernel, own_bins),
        [
            shape((2 * GW, slots), BF16),
            shape((EXTRA, slots), F32),
            shape((2, slots, columns), BF16),
            shape((2, GW, columns), BF16),
        ],
    )(got, got_head)
    upper = lax.ppermute(upper, "bin", [(i, i + 1) for i in range(groups - 1)])
    spectral = call(
        functools.partial(spectral_kernel, own_bins),
        shape((groups, per, 2 * own_bins, columns), BF16),
        grid=(blocks,),
        in_specs=[whole(2 * GW, slots), whole(EXTRA, slots), whole(2, slots, columns)],
        out_specs=pl.BlockSpec(
            (groups // blocks, per, 2 * own_bins, columns), lambda i: (i, 0, 0, 0)
        ),
    )(head, weight, rows)
    spectral = call(
        carry_kernel, shape(spectral.shape, BF16), input_output_aliases={0: 0}
    )(spectral, upper)
    chi = call(
        functools.partial(hilbert_kernel, own_bins),
        shape(spectral.shape, BF16),
        scratch_shapes=[pltpu.VMEM((2 * NB, 2 * NB), BF16)] * 2,
    )(exchange(spectral))
    return call(
        final_kernel,
        shape((own_bins, 2, GW, columns), F32),
        grid=(columns // LANES,),
        in_specs=[
            pl.BlockSpec((groups, per, 2 * own_bins, LANES), lambda i: (0, 0, 0, i))
        ],
        out_specs=pl.BlockSpec((own_bins, 2, GW, LANES), lambda i: (0, 0, 0, i)),
        scratch_shapes=[pltpu.VMEM((GW * 2 * own_bins, LANES), F32)],
    )(exchange(chi))


def solution(mesh):
    placed = (P("bin", None, "gcol"), P("bin", None), P("bin"), P("bin"))
    return jax.shard_map(
        on_device,
        mesh=mesh,
        in_specs=placed,
        out_specs=P("bin", None, None, "gcol"),
        check_vma=False,
    )
```

```python
import functools

import jax
import jax.numpy as jnp
from jax import lax
from jax.experimental import pallas as pl
from jax.experimental.pallas import tpu as pltpu
from jax.sharding import Mesh
from jax.sharding import PartitionSpec as P

NB = 256
GW = 128
LANES = 128
EXTRA = 16
ROW = 8
BIN = ("y", "x", "core")
ORDER = ("x", "y", "core")
BF16 = jnp.bfloat16
F32 = jnp.float32
VMEM_BYTES = 24 * 1024 * 1024


def dot(a, b):
    return jnp.dot(a, b, preferred_element_type=F32)


def iota(shape, axis):
    return lax.broadcasted_iota(jnp.int32, shape, axis)


def call(kernel, out_shape, **options):
    return pl.pallas_call(
        kernel,
        out_shape=out_shape,
        compiler_params=pltpu.CompilerParams(vmem_limit_bytes=VMEM_BYTES),
        **options,
    )


def along_path(index):
    row, at = index // ROW, index % ROW
    return row * ROW + at + (row % 2) * (ROW - 1 - 2 * at)


def block_at(place):
    return place % ROW // 2 * ROW + place // ROW * 2 + place % 2


def slot_onehot(target, slots):
    return (iota((slots, target.shape[1]), 0) == target).astype(F32).astype(BF16)


def tile_rows(tile, part, capacity):
    at = (2 * tile + part) * capacity
    return slice(at, at + capacity)


def pack_rows_kernel(
    quarter_ref, owner_ref, offset_ref, frac_ref, rows_ref, head_ref, target_ref, copy_ref, out_ref
):
    groups, depth, _ = out_ref.shape
    pairs = owner_ref.shape[1]
    tiles = rows_ref.shape[2] // LANES
    capacity = (depth - EXTRA) // (2 * tiles)
    copy_ref[...] = head_ref[...]
    owner = owner_ref[...]
    named = (iota((groups, pairs), 0) == owner).astype(F32)
    before = (iota((pairs, pairs), 0) < iota((pairs, pairs), 1)).astype(F32).astype(BF16)
    rank = jnp.sum(dot(named.astype(BF16), before) * named, axis=0, keepdims=True)
    target = along_path(owner) * capacity + rank.astype(jnp.int32)
    target_ref[...] = target
    onehot = slot_onehot(target, groups * capacity)
    for c in range(2):
        packed = dot(onehot, rows_ref[c]).astype(BF16)
        for tile in range(tiles):
            part = packed[:, tile * LANES : (tile + 1) * LANES]
            out_ref[:, tile_rows(tile, c, capacity)] = part.reshape(groups, capacity, LANES)

    frac = frac_ref[...]
    place = iota((EXTRA, pairs), 0)
    weight = jnp.where(place == offset_ref[...], (1.0 - frac).astype(BF16).astype(F32), 0.0)
    weight += jnp.where(place == offset_ref[...] + 1, frac.astype(BF16).astype(F32), 0.0)
    weight = lax.dot_general(
        weight.astype(BF16), onehot, (((1,), (1,)), ((), ())), preferred_element_type=F32
    )
    share = LANES // capacity
    quarter = quarter_ref[0]
    mine = iota((EXTRA, LANES), 1) // capacity == quarter
    for group in range(groups):
        tile = weight[:, group // share * LANES : (group // share + 1) * LANES]
        turn = (quarter + share - group % share) % share * capacity
        tile = jnp.where(mine, pltpu.roll(tile, turn, 1), 0.0)
        out_ref[group, depth - EXTRA :] = tile.astype(BF16)


def pack_heads_kernel(target_ref, head_ref, arrived_ref, high_ref, low_ref, out_ref):
    groups, double, lanes = out_ref.shape
    capacity = double // 2
    onehot = slot_onehot(target_ref[...], groups * capacity)
    packed = dot(onehot, head_ref[...]).astype(BF16)
    for c in range(2):
        part = packed[:, c * lanes : (c + 1) * lanes]
        out_ref[:, c * capacity : (c + 1) * capacity] = part.reshape(groups, capacity, lanes)


def prepare_kernel(own_bins, got_ref, got_head_ref, head_ref, weight_ref, rows_ref, upper_ref):
    groups, double, lanes = got_head_ref.shape
    capacity = double // 2
    slots = groups * capacity
    share = LANES // capacity
    extra = got_ref.shape[1] - EXTRA
    for c in range(2):
        for tile in range(rows_ref.shape[1] // LANES):
            part = got_ref[:, tile_rows(tile, c, capacity)].reshape(slots, LANES)
            for at in range(c, 3, 2):
                rows_ref[
                    at * slots : (at + 1) * slots, tile * LANES : (tile + 1) * LANES
                ] = part
        head = got_head_ref[:, c * capacity : (c + 1) * capacity].reshape(slots, lanes)
        head_ref[c * lanes : (c + 1) * lanes] = head.astype(F32).T.astype(BF16)
    for at in range(groups // share):
        tile = got_ref[share * at, extra:].astype(F32)
        for k in range(1, share):
            tile += got_ref[share * at + k, extra:].astype(F32)
        weight_ref[:, at * LANES : (at + 1) * LANES] = tile
    weight = weight_ref[own_bins : own_bins + 1]
    scaled = [
        (head_ref[c * GW : (c + 1) * GW].astype(F32) * weight).astype(BF16) for c in range(2)
    ]
    for c, part in enumerate(complex_dot(scaled, rows_ref)):
        upper_ref[c] = part.astype(BF16)


def complex_dot(left, rows_ref):
    slots = rows_ref.shape[0] // 3
    real = dot(jnp.concatenate(left, axis=1), rows_ref[: 2 * slots])
    imag = dot(jnp.concatenate([left[0], -left[1]], axis=1), rows_ref[slots:])
    return real, imag


def spectral_kernel(own_bins, head_ref, weight_ref, rows_ref, out_ref):
    chunk, per, bins, width = out_ref.shape
    window = chunk * per
    slots = weight_ref.shape[1]
    at = pl.program_id(0) * window
    scaled = []
    for c in range(2):
        head = head_ref[pl.ds(pl.multiple_of(c * GW + at, window), window)].astype(F32)
        part = (head[:, None, :] * weight_ref[:own_bins][None]).astype(BF16)
        scaled.append(part.reshape(window * own_bins, slots))
    result = [part.reshape(window, own_bins, width) for part in complex_dot(scaled, rows_ref)]
    result = jnp.concatenate(result, axis=1).reshape(chunk, per, bins, width)
    out_ref[...] = result.astype(BF16)


def carry_kernel(spectral_ref, upper_ref, out_ref):
    groups, per, bins, width = out_ref.shape
    place = iota((groups * per, bins, width), 1)
    values = spectral_ref[...].astype(F32).reshape(groups * per, bins, width)
    for c in range(2):
        upper = upper_ref[c].astype(F32).reshape(groups * per, 1, width)
        values = values + jnp.where(place == c * (bins // 2), upper, 0.0)
    out_ref[...] = values.astype(BF16).reshape(groups, per, bins, width)


def table_kernel(own_bins, high_ref, low_ref):
    shape = high_ref.shape
    row = iota(shape, 0)
    column = iota(shape, 1)
    group = 2 * own_bins
    frequency = (block_at(row // group) * own_bins + row % own_bins).astype(F32)
    bin_at = (along_path(column // group) * own_bins + column % own_bins).astype(F32)
    row_imag = row // own_bins % 2 == 1
    column_imag = column // own_bins % 2 == 1
    difference = frequency - bin_at
    second = frequency + bin_at + 1.0
    first_scale = 1.0 / (difference * difference + 1.0)
    second_scale = 1.0 / (second * second + 1.0)
    real_part = difference * first_scale - second * second_scale
    imag_part = second_scale - first_scale
    crossed = jnp.where(row_imag, imag_part, -imag_part)
    table = jnp.where(row_imag == column_imag, real_part, crossed)
    high = table.astype(BF16)
    high_ref[...] = high
    low_ref[...] = (table - high.astype(F32)).astype(BF16)


def hilbert_kernel(high, low, in_ref, out_ref):
    groups, per, bins, width = out_ref.shape
    for g in range(per):
        values = in_ref[:, g].reshape(groups * bins, width)
        result = dot(high[...], values) + dot(low[...], values)
        out_ref[:, g] = result.astype(BF16).reshape(groups, bins, width)


def final_kernel(in_ref, out_ref, wide):
    groups, per, depth, lanes = in_ref.shape
    wide[...] = in_ref[...].astype(F32).reshape(groups * per * depth, lanes)
    for c in range(2):
        for step in range(depth // 2):
            out_ref[step, c] = wide[
                pl.ds(c * (depth // 2) + step, groups * per, stride=depth), :
            ]


def from_first(block, axis):
    place = lax.axis_index(axis)
    ahead = lax.ppermute(block, axis, [(0, 3)])
    behind = lax.ppermute(block, axis, [(0, 5)])
    block = jnp.where(place == 3, ahead, jnp.where(place == 5, behind, block))
    ahead = lax.ppermute(block, axis, [(0, 1), (3, 4), (5, 6)])
    behind = lax.ppermute(block, axis, [(0, 7), (3, 2)])
    use_ahead = (place == 1) | (place == 4) | (place == 6)
    use_behind = (place == 7) | (place == 2)
    return jnp.where(use_ahead, ahead, jnp.where(use_behind, behind, block))


def exchange(block):
    return lax.all_to_all(block, ORDER, split_axis=0, concat_axis=0, tiled=True)


def on_device(pair_rows, pair_owner, pair_offset, pair_frac):
    groups = lax.axis_size(BIN)
    pairs, _, columns = pair_rows.shape
    capacity = 2 * pairs // groups
    slots = groups * capacity
    own_bins = NB // groups
    per = GW // groups
    blocks = 2
    shape = jax.ShapeDtypeStruct
    scalar = pl.BlockSpec(memory_space=pltpu.SMEM)
    here = pl.BlockSpec(memory_space=pltpu.VMEM)

    quarter = lax.axis_index(ORDER) % (LANES // capacity)
    by_part = jnp.swapaxes(pair_rows, 0, 1)
    target, head, packed = call(
        pack_rows_kernel,
        [
            shape((1, pairs), jnp.int32),
            shape((pairs, 2 * GW), BF16),
            shape((groups, 2 * capacity * columns // LANES + EXTRA, LANES), BF16),
        ],
        in_specs=[scalar] + [here] * 5,
    )(
        quarter.reshape(1),
        pair_owner.reshape(1, pairs),
        pair_offset.reshape(1, pairs),
        pair_frac.reshape(1, pairs),
        by_part,
        pair_rows[:, :, :GW].reshape(pairs, 2 * GW),
    )
    got = exchange(packed)
    head = from_first(head, "gcol")
    high, low = call(
        functools.partial(table_kernel, own_bins), [shape((2 * NB, 2 * NB), BF16)] * 2
    )()
    got_head = exchange(
        call(
            pack_heads_kernel,
            shape((groups, 2 * capacity, GW), BF16),
            in_specs=[here] * 2 + [pl.BlockSpec(memory_space=pl.ANY)] * 3,
        )(target, head, got, high, low)
    )

    whole = lambda *dims: pl.BlockSpec(dims, lambda i: (0,) * len(dims))
    head, weight, rows, upper = call(
        functools.partial(prepare_kernel, own_bins),
        [
            shape((2 * GW, slots), BF16),
            shape((EXTRA, slots), F32),
            shape((3 * slots, columns), BF16),
            shape((2, GW, columns), BF16),
        ],
    )(got, got_head)
    path = [block_at(along_path(i)) for i in range(groups)]
    upper = lax.ppermute(upper, BIN, list(zip(path[:-1], path[1:])))
    spectral = call(
        functools.partial(spectral_kernel, own_bins),
        shape((groups, per, 2 * own_bins, columns), BF16),
        grid=(blocks,),
        in_specs=[whole(2 * GW, slots), whole(EXTRA, slots), whole(3 * slots, columns)],
        out_specs=pl.BlockSpec(
            (groups // blocks, per, 2 * own_bins, columns), lambda i: (i, 0, 0, 0)
        ),
    )(head, weight, rows)
    spectral = call(
        carry_kernel, shape(spectral.shape, BF16), input_output_aliases={0: 0}
    )(spectral, upper)
    chi = call(hilbert_kernel, shape(spectral.shape, BF16))(high, low, exchange(spectral))
    return call(
        final_kernel,
        shape((own_bins, 2, GW, columns), F32),
        grid=(columns // LANES,),
        in_specs=[
            pl.BlockSpec((groups, per, 2 * own_bins, LANES), lambda i: (0, 0, 0, i))
        ],
        out_specs=pl.BlockSpec((own_bins, 2, GW, LANES), lambda i: (0, 0, 0, i)),
        scratch_shapes=[pltpu.VMEM((GW * 2 * own_bins, LANES), F32)],
    )(exchange(chi))


def solution(mesh):
    bins, columns = mesh.devices.shape
    devices = mesh.devices.reshape(bins // ROW, ROW // 2, 2, columns)
    placed = (P(BIN, None, "gcol"), P(BIN, None), P(BIN), P(BIN))
    return jax.shard_map(
        on_device,
        mesh=Mesh(devices, (*BIN, "gcol")),
        in_specs=placed,
        out_specs=P(BIN, None, None, "gcol"),
        check_vma=False,
    )
```

```python
import functools

import jax
import jax.numpy as jnp
from jax import lax
from jax.experimental import pallas as pl
from jax.experimental.pallas import tpu as pltpu
from jax.sharding import Mesh
from jax.sharding import PartitionSpec as P

NB = 256
GW = 128
LANES = 128
EXTRA = 8
WEIGHT_ROWS = 16
ROW = 8
BIN = ("y", "x", "core")
ORDER = ("x", "y", "core")
BF16 = jnp.bfloat16
F32 = jnp.float32
VMEM_BYTES = 24 * 1024 * 1024


def dot(a, b):
    return jnp.dot(a, b, preferred_element_type=F32)


def iota(shape, axis):
    return lax.broadcasted_iota(jnp.int32, shape, axis)


def call(kernel, out_shape, **options):
    return pl.pallas_call(
        kernel,
        out_shape=out_shape,
        compiler_params=pltpu.CompilerParams(vmem_limit_bytes=VMEM_BYTES),
        **options,
    )


def along_path(index):
    row, at = index // ROW, index % ROW
    return row * ROW + at + (row % 2) * (ROW - 1 - 2 * at)


def block_at(place):
    return place % ROW // 2 * ROW + place // ROW * 2 + place % 2


def slot_onehot(target, slots):
    return (iota((slots, target.shape[1]), 0) == target).astype(F32).astype(BF16)


def tile_rows(tile, part, capacity):
    at = (2 * tile + part) * capacity
    return slice(at, at + capacity)


def pack_rows_kernel(
    quarter_ref, owner_ref, offset_ref, frac_ref, rows_ref, head_ref, target_ref, copy_ref, out_ref
):
    groups, depth, _ = out_ref.shape
    pairs = owner_ref.shape[1]
    tiles = rows_ref.shape[2] // LANES
    capacity = (depth - EXTRA) // (2 * tiles)
    copy_ref[...] = head_ref[...]
    owner = owner_ref[...]
    named = (iota((groups, pairs), 0) == owner).astype(F32)
    before = (iota((pairs, pairs), 0) < iota((pairs, pairs), 1)).astype(F32).astype(BF16)
    rank = jnp.sum(dot(named.astype(BF16), before) * named, axis=0, keepdims=True)
    target = along_path(owner) * capacity + rank.astype(jnp.int32)
    target_ref[...] = target
    onehot = slot_onehot(target, groups * capacity)
    for c in range(2):
        packed = dot(onehot, rows_ref[c]).astype(BF16)
        for tile in range(tiles):
            part = packed[:, tile * LANES : (tile + 1) * LANES]
            out_ref[:, tile_rows(tile, c, capacity)] = part.reshape(groups, capacity, LANES)

    frac = frac_ref[...]
    place = iota((EXTRA, pairs), 0)
    weight = jnp.where(place == 0, (1.0 - frac).astype(BF16).astype(F32), 0.0)
    weight = jnp.where(place == 1, frac.astype(BF16).astype(F32), weight)
    weight = jnp.where(place == 2, offset_ref[...].astype(F32), weight)
    weight = lax.dot_general(
        weight.astype(BF16), onehot, (((1,), (1,)), ((), ())), preferred_element_type=F32
    )
    share = LANES // capacity
    quarter = quarter_ref[0]
    mine = iota((EXTRA, LANES), 1) // capacity == quarter
    for group in range(groups):
        tile = weight[:, group // share * LANES : (group // share + 1) * LANES]
        turn = (quarter + share - group % share) % share * capacity
        tile = jnp.where(mine, pltpu.roll(tile, turn, 1), 0.0)
        out_ref[group, depth - EXTRA :] = tile.astype(BF16)


def pack_heads_kernel(target_ref, head_ref, arrived_ref, high_ref, low_ref, out_ref):
    groups, double, lanes = out_ref.shape
    capacity = double // 2
    onehot = slot_onehot(target_ref[...], groups * capacity)
    packed = dot(onehot, head_ref[...]).astype(BF16)
    for c in range(2):
        part = packed[:, c * lanes : (c + 1) * lanes]
        out_ref[:, c * capacity : (c + 1) * capacity] = part.reshape(groups, capacity, lanes)


def prepare_kernel(own_bins, got_ref, got_head_ref, head_ref, weight_ref, rows_ref, upper_ref):
    groups, double, lanes = got_head_ref.shape
    capacity = double // 2
    slots = groups * capacity
    share = LANES // capacity
    extra = got_ref.shape[1] - EXTRA
    for c in range(2):
        for tile in range(rows_ref.shape[1] // LANES):
            part = got_ref[:, tile_rows(tile, c, capacity)].reshape(slots, LANES)
            for at in range(c, 3, 2):
                rows_ref[
                    at * slots : (at + 1) * slots, tile * LANES : (tile + 1) * LANES
                ] = part
        head = got_head_ref[:, c * capacity : (c + 1) * capacity].reshape(slots, lanes)
        head_ref[c * lanes : (c + 1) * lanes] = head.astype(F32).T.astype(BF16)
    for at in range(groups // share):
        tile = got_ref[share * at, extra:].astype(F32)
        for k in range(1, share):
            tile += got_ref[share * at + k, extra:].astype(F32)
        low, high, offset = (tile[n : n + 1] for n in range(3))
        place = iota((WEIGHT_ROWS, LANES), 0).astype(F32)
        weight = jnp.where(place == offset, low, 0.0) + jnp.where(place == offset + 1.0, high, 0.0)
        weight_ref[:, at * LANES : (at + 1) * LANES] = weight
    weight = weight_ref[own_bins : own_bins + 1]
    scaled = [
        (head_ref[c * GW : (c + 1) * GW].astype(F32) * weight).astype(BF16) for c in range(2)
    ]
    for c, part in enumerate(complex_dot(scaled, rows_ref)):
        upper_ref[c] = part.astype(BF16)


def complex_dot(left, rows_ref):
    slots = rows_ref.shape[0] // 3
    real = dot(jnp.concatenate(left, axis=1), rows_ref[: 2 * slots])
    imag = dot(jnp.concatenate([left[0], -left[1]], axis=1), rows_ref[slots:])
    return real, imag


def spectral_kernel(own_bins, head_ref, weight_ref, rows_ref, out_ref):
    chunk, per, bins, width = out_ref.shape
    window = chunk * per
    slots = weight_ref.shape[1]
    at = pl.program_id(0) * window
    scaled = []
    for c in range(2):
        head = head_ref[pl.ds(pl.multiple_of(c * GW + at, window), window)].astype(F32)
        part = (head[:, None, :] * weight_ref[:own_bins][None]).astype(BF16)
        scaled.append(part.reshape(window * own_bins, slots))
    result = [part.reshape(window, own_bins, width) for part in complex_dot(scaled, rows_ref)]
    result = jnp.concatenate(result, axis=1).reshape(chunk, per, bins, width)
    out_ref[...] = result.astype(BF16)


def carry_kernel(spectral_ref, upper_ref, out_ref):
    groups, per, bins, width = out_ref.shape
    place = iota((groups * per, bins, width), 1)
    values = spectral_ref[...].astype(F32).reshape(groups * per, bins, width)
    for c in range(2):
        upper = upper_ref[c].astype(F32).reshape(groups * per, 1, width)
        values = values + jnp.where(place == c * (bins // 2), upper, 0.0)
    out_ref[...] = values.astype(BF16).reshape(groups, per, bins, width)


def table_kernel(own_bins, high_ref, low_ref):
    shape = high_ref.shape
    row = iota(shape, 0)
    column = iota(shape, 1)
    group = 2 * own_bins
    frequency = (block_at(row // group) * own_bins + row % own_bins).astype(F32)
    bin_at = (along_path(column // group) * own_bins + column % own_bins).astype(F32)
    row_imag = row // own_bins % 2 == 1
    column_imag = column // own_bins % 2 == 1
    difference = frequency - bin_at
    second = frequency + bin_at + 1.0
    first_scale = 1.0 / (difference * difference + 1.0)
    second_scale = 1.0 / (second * second + 1.0)
    real_part = difference * first_scale - second * second_scale
    imag_part = second_scale - first_scale
    crossed = jnp.where(row_imag, imag_part, -imag_part)
    table = jnp.where(row_imag == column_imag, real_part, crossed)
    high = table.astype(BF16)
    high_ref[...] = high
    low_ref[...] = (table - high.astype(F32)).astype(BF16)


def hilbert_kernel(high, low, in_ref, out_ref):
    groups, per, bins, width = out_ref.shape
    for g in range(per):
        values = in_ref[:, g].reshape(groups * bins, width)
        result = dot(high[...], values) + dot(low[...], values)
        out_ref[:, g] = result.astype(BF16).reshape(groups, bins, width)


def final_kernel(in_ref, out_ref, wide):
    groups, per, depth, lanes = in_ref.shape
    for k in range(lanes // LANES):
        at = slice(k * LANES, (k + 1) * LANES)
        wide[k] = in_ref[:, :, :, at].astype(F32).reshape(groups * per * depth, LANES)
        for c in range(2):
            for step in range(depth // 2):
                out_ref[step, c, :, at] = wide[
                    k, pl.ds(c * (depth // 2) + step, groups * per, stride=depth), :
                ]


def from_first(block, axis):
    place = lax.axis_index(axis)
    ahead = lax.ppermute(block, axis, [(0, 3)])
    behind = lax.ppermute(block, axis, [(0, 5)])
    block = jnp.where(place == 3, ahead, jnp.where(place == 5, behind, block))
    ahead = lax.ppermute(block, axis, [(0, 1), (3, 4), (5, 6)])
    behind = lax.ppermute(block, axis, [(0, 7), (3, 2)])
    use_ahead = (place == 1) | (place == 4) | (place == 6)
    use_behind = (place == 7) | (place == 2)
    return jnp.where(use_ahead, ahead, jnp.where(use_behind, behind, block))


def exchange(block):
    return lax.all_to_all(block, ORDER, split_axis=0, concat_axis=0, tiled=True)


def on_device(pair_rows, pair_owner, pair_offset, pair_frac):
    groups = lax.axis_size(BIN)
    pairs, _, columns = pair_rows.shape
    capacity = 2 * pairs // groups
    slots = groups * capacity
    own_bins = NB // groups
    per = GW // groups
    blocks = 1
    shape = jax.ShapeDtypeStruct
    scalar = pl.BlockSpec(memory_space=pltpu.SMEM)
    here = pl.BlockSpec(memory_space=pltpu.VMEM)

    quarter = lax.axis_index(ORDER) % (LANES // capacity)
    by_part = jnp.swapaxes(pair_rows, 0, 1)
    target, head, packed = call(
        pack_rows_kernel,
        [
            shape((1, pairs), jnp.int32),
            shape((pairs, 2 * GW), BF16),
            shape((groups, 2 * capacity * columns // LANES + EXTRA, LANES), BF16),
        ],
        in_specs=[scalar] + [here] * 5,
    )(
        quarter.reshape(1),
        pair_owner.reshape(1, pairs),
        pair_offset.reshape(1, pairs),
        pair_frac.reshape(1, pairs),
        by_part,
        pair_rows[:, :, :GW].reshape(pairs, 2 * GW),
    )
    got = exchange(packed)
    head = from_first(head, "gcol")
    high, low = call(
        functools.partial(table_kernel, own_bins), [shape((2 * NB, 2 * NB), BF16)] * 2
    )()
    got_head = exchange(
        call(
            pack_heads_kernel,
            shape((groups, 2 * capacity, GW), BF16),
            in_specs=[here] * 2 + [pl.BlockSpec(memory_space=pl.ANY)] * 3,
        )(target, head, got, high, low)
    )

    whole = lambda *dims: pl.BlockSpec(dims, lambda i: (0,) * len(dims))
    head, weight, rows, upper = call(
        functools.partial(prepare_kernel, own_bins),
        [
            shape((2 * GW, slots), BF16),
            shape((WEIGHT_ROWS, slots), F32),
            shape((3 * slots, columns), BF16),
            shape((2, GW, columns), BF16),
        ],
    )(got, got_head)
    path = [block_at(along_path(i)) for i in range(groups)]
    upper = lax.ppermute(upper, BIN, list(zip(path[:-1], path[1:])))
    spectral = call(
        functools.partial(spectral_kernel, own_bins),
        shape((groups, per, 2 * own_bins, columns), BF16),
        grid=(blocks,),
        in_specs=[whole(2 * GW, slots), whole(WEIGHT_ROWS, slots), whole(3 * slots, columns)],
        out_specs=pl.BlockSpec(
            (groups // blocks, per, 2 * own_bins, columns), lambda i: (i, 0, 0, 0)
        ),
    )(head, weight, rows)
    spectral = call(
        carry_kernel, shape(spectral.shape, BF16), input_output_aliases={0: 0}
    )(spectral, upper)
    chi = call(hilbert_kernel, shape(spectral.shape, BF16))(high, low, exchange(spectral))
    return call(
        final_kernel,
        shape((own_bins, 2, GW, columns), F32),
        grid=(2,),
        in_specs=[
            pl.BlockSpec((groups, per, 2 * own_bins, columns // 2), lambda i: (0, 0, 0, i))
        ],
        out_specs=pl.BlockSpec((own_bins, 2, GW, columns // 2), lambda i: (0, 0, 0, i)),
        scratch_shapes=[pltpu.VMEM((columns // LANES // 2, GW * 2 * own_bins, LANES), F32)],
    )(exchange(chi))


def solution(mesh):
    bins, columns = mesh.devices.shape
    devices = mesh.devices.reshape(bins // ROW, ROW // 2, 2, columns)
    placed = (P(BIN, None, "gcol"), P(BIN, None), P(BIN), P(BIN))
    return jax.shard_map(
        on_device,
        mesh=Mesh(devices, (*BIN, "gcol")),
        in_specs=placed,
        out_specs=P(BIN, None, None, "gcol"),
        check_vma=False,
    )
```

```python
import functools

import jax
import jax.numpy as jnp
from jax import lax
from jax.experimental import pallas as pl
from jax.experimental.pallas import tpu as pltpu
from jax.sharding import Mesh
from jax.sharding import PartitionSpec as P

NB = 256
GW = 128
LANES = 128
EXTRA = 8
WEIGHT_ROWS = 16
ROW = 8
BIN = ("y", "x", "core")
ORDER = ("x", "y", "core")
BF16 = jnp.bfloat16
F32 = jnp.float32
VMEM_BYTES = 24 * 1024 * 1024


def dot(a, b):
    return jnp.dot(a, b, preferred_element_type=F32)


def iota(shape, axis):
    return lax.broadcasted_iota(jnp.int32, shape, axis)


def call(kernel, out_shape, **options):
    return pl.pallas_call(
        kernel,
        out_shape=out_shape,
        compiler_params=pltpu.CompilerParams(vmem_limit_bytes=VMEM_BYTES),
        **options,
    )


def along_path(index):
    row, at = index // ROW, index % ROW
    return row * ROW + at + (row % 2) * (ROW - 1 - 2 * at)


def block_at(place):
    return place % ROW // 2 * ROW + place // ROW * 2 + place % 2


def slot_onehot(target, slots):
    return (iota((slots, target.shape[1]), 0) == target).astype(F32).astype(BF16)


def tile_rows(tile, part, capacity):
    at = (2 * tile + part) * capacity
    return slice(at, at + capacity)


def pack_rows_kernel(
    quarter_ref, owner_ref, offset_ref, frac_ref, rows_ref, head_ref, target_ref, copy_ref, out_ref
):
    groups, depth, _ = out_ref.shape
    pairs = owner_ref.shape[1]
    tiles = rows_ref.shape[2] // LANES
    capacity = (depth - EXTRA) // (2 * tiles)
    copy_ref[...] = head_ref[...]
    owner = owner_ref[...]
    named = (iota((groups, pairs), 0) == owner).astype(F32)
    before = (iota((pairs, pairs), 0) < iota((pairs, pairs), 1)).astype(F32).astype(BF16)
    rank = jnp.sum(dot(named.astype(BF16), before) * named, axis=0, keepdims=True)
    target = along_path(owner) * capacity + rank.astype(jnp.int32)
    target_ref[...] = target
    onehot = slot_onehot(target, groups * capacity)
    for c in range(2):
        packed = dot(onehot, rows_ref[c]).astype(BF16)
        for tile in range(tiles):
            part = packed[:, tile * LANES : (tile + 1) * LANES]
            out_ref[:, tile_rows(tile, c, capacity)] = part.reshape(groups, capacity, LANES)

    frac = frac_ref[...]
    place = iota((EXTRA, pairs), 0)
    weight = jnp.where(place == 0, (1.0 - frac).astype(BF16).astype(F32), 0.0)
    inside = owner * (NB // groups) + offset_ref[...] < NB - 1
    weight = jnp.where((place == 1) & inside, frac.astype(BF16).astype(F32), weight)
    weight = jnp.where(place == 2, offset_ref[...].astype(F32), weight)
    weight = lax.dot_general(
        weight.astype(BF16), onehot, (((1,), (1,)), ((), ())), preferred_element_type=F32
    )
    share = LANES // capacity
    quarter = quarter_ref[0]
    mine = iota((EXTRA, LANES), 1) // capacity == quarter
    for group in range(groups):
        tile = weight[:, group // share * LANES : (group // share + 1) * LANES]
        turn = (quarter + share - group % share) % share * capacity
        tile = jnp.where(mine, pltpu.roll(tile, turn, 1), 0.0)
        out_ref[group, depth - EXTRA :] = tile.astype(BF16)


def pack_heads_kernel(target_ref, head_ref, arrived_ref, high_ref, low_ref, out_ref):
    groups, double, lanes = out_ref.shape
    capacity = double // 2
    onehot = slot_onehot(target_ref[...], groups * capacity)
    packed = dot(onehot, head_ref[...]).astype(BF16)
    for c in range(2):
        part = packed[:, c * lanes : (c + 1) * lanes]
        out_ref[:, c * capacity : (c + 1) * capacity] = part.reshape(groups, capacity, lanes)


def prepare_kernel(own_bins, got_ref, got_head_ref, head_ref, weight_ref, rows_ref, upper_ref):
    groups, double, lanes = got_head_ref.shape
    capacity = double // 2
    slots = groups * capacity
    share = LANES // capacity
    extra = got_ref.shape[1] - EXTRA
    for c in range(2):
        for tile in range(rows_ref.shape[1] // LANES):
            part = got_ref[:, tile_rows(tile, c, capacity)].reshape(slots, LANES)
            for at in range(c, 3, 2):
                rows_ref[
                    at * slots : (at + 1) * slots, tile * LANES : (tile + 1) * LANES
                ] = part
        head = got_head_ref[:, c * capacity : (c + 1) * capacity].reshape(slots, lanes)
        head_ref[c * lanes : (c + 1) * lanes] = head.astype(F32).T.astype(BF16)
    for at in range(groups // share):
        tile = got_ref[share * at, extra:].astype(F32)
        for k in range(1, share):
            tile += got_ref[share * at + k, extra:].astype(F32)
        low, high, offset = (tile[n : n + 1] for n in range(3))
        place = iota((WEIGHT_ROWS, LANES), 0).astype(F32)
        weight = jnp.where(place == offset, low, 0.0) + jnp.where(place == offset + 1.0, high, 0.0)
        weight_ref[:, at * LANES : (at + 1) * LANES] = weight
    weight = weight_ref[own_bins : own_bins + 1]
    scaled = [
        (head_ref[c * GW : (c + 1) * GW].astype(F32) * weight).astype(BF16) for c in range(2)
    ]
    for c, part in enumerate(complex_dot(scaled, rows_ref)):
        upper_ref[c] = part.astype(BF16)


def complex_dot(left, rows_ref):
    slots = rows_ref.shape[0] // 3
    real = dot(jnp.concatenate(left, axis=1), rows_ref[: 2 * slots])
    imag = dot(jnp.concatenate([left[0], -left[1]], axis=1), rows_ref[slots:])
    return real, imag


def spectral_kernel(own_bins, head_ref, weight_ref, rows_ref, out_ref):
    chunk, per, bins, width = out_ref.shape
    window = chunk * per
    slots = weight_ref.shape[1]
    at = pl.program_id(0) * window
    scaled = []
    for c in range(2):
        head = head_ref[pl.ds(pl.multiple_of(c * GW + at, window), window)].astype(F32)
        part = (head[:, None, :] * weight_ref[:own_bins][None]).astype(BF16)
        scaled.append(part.reshape(window * own_bins, slots))
    result = [part.reshape(window, own_bins, width) for part in complex_dot(scaled, rows_ref)]
    result = jnp.concatenate(result, axis=1).reshape(chunk, per, bins, width)
    out_ref[...] = result.astype(BF16)


def carry_kernel(spectral_ref, upper_ref, out_ref):
    groups, per, bins, width = out_ref.shape
    place = iota((groups * per, bins, width), 1)
    values = spectral_ref[...].astype(F32).reshape(groups * per, bins, width)
    for c in range(2):
        upper = upper_ref[c].astype(F32).reshape(groups * per, 1, width)
        values = values + jnp.where(place == c * (bins // 2), upper, 0.0)
    out_ref[...] = values.astype(BF16).reshape(groups, per, bins, width)


def table_kernel(own_bins, high_ref, low_ref):
    shape = high_ref.shape
    row = iota(shape, 0)
    column = iota(shape, 1)
    group = 2 * own_bins
    frequency = (block_at(row // group) * own_bins + row % own_bins).astype(F32)
    bin_at = (along_path(column // group) * own_bins + column % own_bins).astype(F32)
    row_imag = row // own_bins % 2 == 1
    column_imag = column // own_bins % 2 == 1
    difference = frequency - bin_at
    second = frequency + bin_at + 1.0
    first_scale = 1.0 / (difference * difference + 1.0)
    second_scale = 1.0 / (second * second + 1.0)
    real_part = difference * first_scale - second * second_scale
    imag_part = second_scale - first_scale
    crossed = jnp.where(row_imag, imag_part, -imag_part)
    table = jnp.where(row_imag == column_imag, real_part, crossed)
    high = table.astype(BF16)
    high_ref[...] = high
    low_ref[...] = (table - high.astype(F32)).astype(BF16)


def hilbert_kernel(high, low, in_ref, out_ref):
    groups, per, bins, width = out_ref.shape
    for g in range(per):
        values = in_ref[:, g].reshape(groups * bins, width)
        result = dot(high[...], values) + dot(low[...], values)
        out_ref[:, g] = result.astype(BF16).reshape(groups, bins, width)


def final_kernel(in_ref, out_ref, wide):
    groups, per, depth, lanes = in_ref.shape
    for k in range(lanes // LANES):
        at = slice(k * LANES, (k + 1) * LANES)
        wide[k] = in_ref[:, :, :, at].astype(F32).reshape(groups * per * depth, LANES)
        for c in range(2):
            for step in range(depth // 2):
                out_ref[step, c, :, at] = wide[
                    k, pl.ds(c * (depth // 2) + step, groups * per, stride=depth), :
                ]


def from_first(block, axis):
    place = lax.axis_index(axis)
    ahead = lax.ppermute(block, axis, [(0, 3)])
    behind = lax.ppermute(block, axis, [(0, 5)])
    block = jnp.where(place == 3, ahead, jnp.where(place == 5, behind, block))
    ahead = lax.ppermute(block, axis, [(0, 1), (3, 4), (5, 6)])
    behind = lax.ppermute(block, axis, [(0, 7), (3, 2)])
    use_ahead = (place == 1) | (place == 4) | (place == 6)
    use_behind = (place == 7) | (place == 2)
    return jnp.where(use_ahead, ahead, jnp.where(use_behind, behind, block))


def exchange(block):
    return lax.all_to_all(block, ORDER, split_axis=0, concat_axis=0, tiled=True)


def on_device(pair_rows, pair_owner, pair_offset, pair_frac):
    groups = lax.axis_size(BIN)
    pairs, _, columns = pair_rows.shape
    capacity = 2 * pairs // groups
    slots = groups * capacity
    own_bins = NB // groups
    per = GW // groups
    blocks = 1
    shape = jax.ShapeDtypeStruct
    scalar = pl.BlockSpec(memory_space=pltpu.SMEM)
    here = pl.BlockSpec(memory_space=pltpu.VMEM)

    quarter = lax.axis_index(ORDER) % (LANES // capacity)
    by_part = jnp.swapaxes(pair_rows, 0, 1)
    target, head, packed = call(
        pack_rows_kernel,
        [
            shape((1, pairs), jnp.int32),
            shape((pairs, 2 * GW), BF16),
            shape((groups, 2 * capacity * columns // LANES + EXTRA, LANES), BF16),
        ],
        in_specs=[scalar] + [here] * 5,
    )(
        quarter.reshape(1),
        pair_owner.reshape(1, pairs),
        pair_offset.reshape(1, pairs),
        pair_frac.reshape(1, pairs),
        by_part,
        pair_rows[:, :, :GW].reshape(pairs, 2 * GW),
    )
    got = exchange(packed)
    head = from_first(head, "gcol")
    high, low = call(
        functools.partial(table_kernel, own_bins), [shape((2 * NB, 2 * NB), BF16)] * 2
    )()
    got_head = exchange(
        call(
            pack_heads_kernel,
            shape((groups, 2 * capacity, GW), BF16),
            in_specs=[here] * 2 + [pl.BlockSpec(memory_space=pl.ANY)] * 3,
        )(target, head, got, high, low)
    )

    whole = lambda *dims: pl.BlockSpec(dims, lambda i: (0,) * len(dims))
    head, weight, rows, upper = call(
        functools.partial(prepare_kernel, own_bins),
        [
            shape((2 * GW, slots), BF16),
            shape((WEIGHT_ROWS, slots), F32),
            shape((3 * slots, columns), BF16),
            shape((2, GW, columns), BF16),
        ],
    )(got, got_head)
    path = [block_at(along_path(i)) for i in range(groups)]
    upper = lax.ppermute(upper, BIN, list(zip(path, path[1:] + path[:1])))
    spectral = call(
        functools.partial(spectral_kernel, own_bins),
        shape((groups, per, 2 * own_bins, columns), BF16),
        grid=(blocks,),
        in_specs=[whole(2 * GW, slots), whole(WEIGHT_ROWS, slots), whole(3 * slots, columns)],
        out_specs=pl.BlockSpec(
            (groups // blocks, per, 2 * own_bins, columns), lambda i: (i, 0, 0, 0)
        ),
    )(head, weight, rows)
    spectral = call(
        carry_kernel, shape(spectral.shape, BF16), input_output_aliases={0: 0}
    )(spectral, upper)
    chi = call(hilbert_kernel, shape(spectral.shape, BF16))(high, low, exchange(spectral))
    return call(
        final_kernel,
        shape((own_bins, 2, GW, columns), F32),
        grid=(2,),
        in_specs=[
            pl.BlockSpec((groups, per, 2 * own_bins, columns // 2), lambda i: (0, 0, 0, i))
        ],
        out_specs=pl.BlockSpec((own_bins, 2, GW, columns // 2), lambda i: (0, 0, 0, i)),
        scratch_shapes=[pltpu.VMEM((columns // LANES // 2, GW * 2 * own_bins, LANES), F32)],
    )(exchange(chi))


def solution(mesh):
    bins, columns = mesh.devices.shape
    devices = mesh.devices.reshape(bins // ROW, ROW // 2, 2, columns)
    placed = (P(BIN, None, "gcol"), P(BIN, None), P(BIN), P(BIN))
    return jax.shard_map(
        on_device,
        mesh=Mesh(devices, (*BIN, "gcol")),
        in_specs=placed,
        out_specs=P(BIN, None, None, "gcol"),
        check_vma=False,
    )
```

```python
import functools

import jax
import jax.numpy as jnp
from jax import lax
from jax.experimental import pallas as pl
from jax.experimental.pallas import tpu as pltpu
from jax.sharding import Mesh
from jax.sharding import PartitionSpec as P

NB = 256
GW = 128
LANES = 128
EXTRA = 8
WEIGHT_ROWS = 16
ROW = 8
BIN = ("y", "x", "core")
ORDER = ("x", "y", "core")
BF16 = jnp.bfloat16
F32 = jnp.float32
VMEM_BYTES = 24 * 1024 * 1024


def dot(a, b):
    return jnp.dot(a, b, preferred_element_type=F32)


def iota(shape, axis):
    return lax.broadcasted_iota(jnp.int32, shape, axis)


def call(kernel, out_shape, **options):
    return pl.pallas_call(
        kernel,
        out_shape=out_shape,
        compiler_params=pltpu.CompilerParams(vmem_limit_bytes=VMEM_BYTES),
        **options,
    )


def along_path(index):
    row, at = index // ROW, index % ROW
    return row * ROW + at + (row % 2) * (ROW - 1 - 2 * at)


def block_at(place):
    return place % ROW // 2 * ROW + place // ROW * 2 + place % 2


def slot_onehot(target, slots):
    return (iota((slots, target.shape[1]), 0) == target).astype(F32).astype(BF16)


def tile_rows(tile, part, capacity):
    at = (2 * tile + part) * capacity
    return slice(at, at + capacity)


def pack_rows_kernel(
    quarter_ref, owner_ref, offset_ref, frac_ref, rows_ref, target_ref, copy_ref, out_ref
):
    groups, depth, _ = out_ref.shape
    pairs = owner_ref.shape[1]
    tiles = rows_ref.shape[2] // LANES
    capacity = (depth - EXTRA) // (2 * tiles)
    for c in range(2):
        copy_ref[:, c * GW : (c + 1) * GW] = rows_ref[c, :, :GW]
    owner = owner_ref[...]
    named = (iota((groups, pairs), 0) == owner).astype(F32)
    before = (iota((pairs, pairs), 0) < iota((pairs, pairs), 1)).astype(F32).astype(BF16)
    rank = jnp.sum(dot(named.astype(BF16), before) * named, axis=0, keepdims=True)
    target = along_path(owner) * capacity + rank.astype(jnp.int32)
    target_ref[...] = target
    onehot = slot_onehot(target, groups * capacity)
    for c in range(2):
        packed = dot(onehot, rows_ref[c]).astype(BF16)
        for tile in range(tiles):
            part = packed[:, tile * LANES : (tile + 1) * LANES]
            out_ref[:, tile_rows(tile, c, capacity)] = part.reshape(groups, capacity, LANES)

    frac = frac_ref[...]
    place = iota((EXTRA, pairs), 0)
    weight = jnp.where(place == 0, (1.0 - frac).astype(BF16).astype(F32), 0.0)
    inside = owner * (NB // groups) + offset_ref[...] < NB - 1
    weight = jnp.where((place == 1) & inside, frac.astype(BF16).astype(F32), weight)
    weight = jnp.where(place == 2, offset_ref[...].astype(F32), weight)
    weight = lax.dot_general(
        weight.astype(BF16), onehot, (((1,), (1,)), ((), ())), preferred_element_type=F32
    )
    share = LANES // capacity
    quarter = quarter_ref[0]
    mine = iota((EXTRA, LANES), 1) // capacity == quarter
    for group in range(groups):
        tile = weight[:, group // share * LANES : (group // share + 1) * LANES]
        turn = (quarter + share - group % share) % share * capacity
        tile = jnp.where(mine, pltpu.roll(tile, turn, 1), 0.0)
        out_ref[group, depth - EXTRA :] = tile.astype(BF16)


def pack_heads_kernel(target_ref, head_ref, arrived_ref, high_ref, low_ref, out_ref):
    groups, double, lanes = out_ref.shape
    capacity = double // 2
    onehot = slot_onehot(target_ref[...], groups * capacity)
    packed = dot(onehot, head_ref[...]).astype(BF16)
    for c in range(2):
        part = packed[:, c * lanes : (c + 1) * lanes]
        out_ref[:, c * capacity : (c + 1) * capacity] = part.reshape(groups, capacity, lanes)


def prepare_kernel(own_bins, got_ref, got_head_ref, head_ref, weight_ref, rows_ref, upper_ref):
    groups, double, lanes = got_head_ref.shape
    capacity = double // 2
    slots = groups * capacity
    share = LANES // capacity
    extra = got_ref.shape[1] - EXTRA
    for c in range(2):
        for tile in range(rows_ref.shape[1] // LANES):
            part = got_ref[:, tile_rows(tile, c, capacity)].reshape(slots, LANES)
            for at in range(c, 3, 2):
                rows_ref[
                    at * slots : (at + 1) * slots, tile * LANES : (tile + 1) * LANES
                ] = part
        head = got_head_ref[:, c * capacity : (c + 1) * capacity].reshape(slots, lanes)
        head_ref[c * lanes : (c + 1) * lanes] = head.astype(F32).T.astype(BF16)
    for at in range(groups // share):
        tile = got_ref[share * at, extra:].astype(F32)
        for k in range(1, share):
            tile += got_ref[share * at + k, extra:].astype(F32)
        low, high, offset = (tile[n : n + 1] for n in range(3))
        place = iota((WEIGHT_ROWS, LANES), 0).astype(F32)
        weight = jnp.where(place == offset, low, 0.0) + jnp.where(place == offset + 1.0, high, 0.0)
        weight_ref[:, at * LANES : (at + 1) * LANES] = weight
    weight = weight_ref[own_bins : own_bins + 1]
    scaled = [
        (head_ref[c * GW : (c + 1) * GW].astype(F32) * weight).astype(BF16) for c in range(2)
    ]
    for c, part in enumerate(complex_dot(scaled, rows_ref)):
        upper_ref[c] = part.astype(BF16)


def complex_dot(left, rows_ref):
    slots = rows_ref.shape[0] // 3
    real = dot(jnp.concatenate(left, axis=1), rows_ref[: 2 * slots])
    imag = dot(jnp.concatenate([left[0], -left[1]], axis=1), rows_ref[slots:])
    return real, imag


def spectral_kernel(own_bins, head_ref, weight_ref, rows_ref, out_ref):
    chunk, per, bins, width = out_ref.shape
    window = chunk * per
    slots = weight_ref.shape[1]
    at = pl.program_id(0) * window
    scaled = []
    for c in range(2):
        head = head_ref[pl.ds(pl.multiple_of(c * GW + at, window), window)].astype(F32)
        part = (head[:, None, :] * weight_ref[:own_bins][None]).astype(BF16)
        scaled.append(part.reshape(window * own_bins, slots))
    result = [part.reshape(window, own_bins, width) for part in complex_dot(scaled, rows_ref)]
    result = jnp.concatenate(result, axis=1).reshape(chunk, per, bins, width)
    out_ref[...] = result.astype(BF16)


def carry_kernel(spectral_ref, upper_ref, out_ref):
    groups, per, bins, width = out_ref.shape
    place = iota((groups * per, bins, width), 1)
    added = jnp.zeros((groups * per, bins, width), F32)
    for c in range(2):
        upper = upper_ref[c].astype(F32).reshape(groups * per, 1, width)
        added = jnp.where(place == c * (bins // 2), upper, added)
    values = spectral_ref[...].reshape(groups * per, bins, width) + added.astype(BF16)
    out_ref[...] = values.reshape(groups, per, bins, width)


def table_kernel(own_bins, high_ref, low_ref):
    shape = high_ref.shape
    row = iota(shape, 0)
    column = iota(shape, 1)
    group = 2 * own_bins
    frequency = (block_at(row // group) * own_bins + row % own_bins).astype(F32)
    bin_at = (along_path(column // group) * own_bins + column % own_bins).astype(F32)
    row_imag = row // own_bins % 2 == 1
    column_imag = column // own_bins % 2 == 1
    difference = frequency - bin_at
    second = frequency + bin_at + 1.0
    first_scale = 1.0 / (difference * difference + 1.0)
    second_scale = 1.0 / (second * second + 1.0)
    real_part = difference * first_scale - second * second_scale
    imag_part = second_scale - first_scale
    crossed = jnp.where(row_imag, imag_part, -imag_part)
    table = jnp.where(row_imag == column_imag, real_part, crossed)
    high = table.astype(BF16)
    high_ref[...] = high
    low_ref[...] = (table - high.astype(F32)).astype(BF16)


def hilbert_kernel(high, low, in_ref, out_ref):
    groups, per, bins, width = out_ref.shape
    for g in range(per):
        values = in_ref[:, g].reshape(groups * bins, width)
        result = dot(high[...], values) + dot(low[...], values)
        out_ref[:, g] = result.astype(BF16).reshape(groups, bins, width)


def final_kernel(in_ref, out_ref, wide):
    groups, per, depth, lanes = in_ref.shape
    for k in range(lanes // LANES):
        at = slice(k * LANES, (k + 1) * LANES)
        wide[k] = in_ref[:, :, :, at].astype(F32).reshape(groups * per * depth, LANES)
        for c in range(2):
            for step in range(depth // 2):
                out_ref[step, c, :, at] = wide[
                    k, pl.ds(c * (depth // 2) + step, groups * per, stride=depth), :
                ]


def from_first(block, axis):
    place = lax.axis_index(axis)
    ahead = lax.ppermute(block, axis, [(0, 3)])
    behind = lax.ppermute(block, axis, [(0, 5)])
    block = jnp.where(place == 3, ahead, jnp.where(place == 5, behind, block))
    ahead = lax.ppermute(block, axis, [(0, 1), (3, 4), (5, 6)])
    behind = lax.ppermute(block, axis, [(0, 7), (3, 2)])
    use_ahead = (place == 1) | (place == 4) | (place == 6)
    use_behind = (place == 7) | (place == 2)
    return jnp.where(use_ahead, ahead, jnp.where(use_behind, behind, block))


def exchange(block):
    return lax.all_to_all(block, ORDER, split_axis=0, concat_axis=0, tiled=True)


def on_device(pair_rows, pair_owner, pair_offset, pair_frac):
    groups = lax.axis_size(BIN)
    pairs, _, columns = pair_rows.shape
    capacity = 2 * pairs // groups
    slots = groups * capacity
    own_bins = NB // groups
    per = GW // groups
    blocks = 1
    shape = jax.ShapeDtypeStruct
    scalar = pl.BlockSpec(memory_space=pltpu.SMEM)
    here = pl.BlockSpec(memory_space=pltpu.VMEM)

    quarter = lax.axis_index(ORDER) % (LANES // capacity)
    by_part = jnp.swapaxes(pair_rows, 0, 1)
    target, head, packed = call(
        pack_rows_kernel,
        [
            shape((1, pairs), jnp.int32),
            shape((pairs, 2 * GW), BF16),
            shape((groups, 2 * capacity * columns // LANES + EXTRA, LANES), BF16),
        ],
        in_specs=[scalar] + [here] * 4,
    )(
        quarter.reshape(1),
        pair_owner.reshape(1, pairs),
        pair_offset.reshape(1, pairs),
        pair_frac.reshape(1, pairs),
        by_part,
    )
    got = exchange(packed)
    head = from_first(head, "gcol")
    high, low = call(
        functools.partial(table_kernel, own_bins), [shape((2 * NB, 2 * NB), BF16)] * 2
    )()
    got_head = exchange(
        call(
            pack_heads_kernel,
            shape((groups, 2 * capacity, GW), BF16),
            in_specs=[here] * 2 + [pl.BlockSpec(memory_space=pl.ANY)] * 3,
        )(target, head, got, high, low)
    )

    whole = lambda *dims: pl.BlockSpec(dims, lambda i: (0,) * len(dims))
    head, weight, rows, upper = call(
        functools.partial(prepare_kernel, own_bins),
        [
            shape((2 * GW, slots), BF16),
            shape((WEIGHT_ROWS, slots), F32),
            shape((3 * slots, columns), BF16),
            shape((2, GW, columns), BF16),
        ],
    )(got, got_head)
    path = [block_at(along_path(i)) for i in range(groups)]
    upper = lax.ppermute(upper, BIN, list(zip(path, path[1:] + path[:1])))
    spectral = call(
        functools.partial(spectral_kernel, own_bins),
        shape((groups, per, 2 * own_bins, columns), BF16),
        grid=(blocks,),
        in_specs=[whole(2 * GW, slots), whole(WEIGHT_ROWS, slots), whole(3 * slots, columns)],
        out_specs=pl.BlockSpec(
            (groups // blocks, per, 2 * own_bins, columns), lambda i: (i, 0, 0, 0)
        ),
    )(head, weight, rows)
    spectral = call(
        carry_kernel, shape(spectral.shape, BF16), input_output_aliases={0: 0}
    )(spectral, upper)
    chi = call(hilbert_kernel, shape(spectral.shape, BF16))(high, low, exchange(spectral))
    return call(
        final_kernel,
        shape((own_bins, 2, GW, columns), F32),
        grid=(2,),
        in_specs=[
            pl.BlockSpec((groups, per, 2 * own_bins, columns // 2), lambda i: (0, 0, 0, i))
        ],
        out_specs=pl.BlockSpec((own_bins, 2, GW, columns // 2), lambda i: (0, 0, 0, i)),
        scratch_shapes=[pltpu.VMEM((columns // LANES // 2, GW * 2 * own_bins, LANES), F32)],
    )(exchange(chi))


def solution(mesh):
    bins, columns = mesh.devices.shape
    devices = mesh.devices.reshape(bins // ROW, ROW // 2, 2, columns)
    placed = (P(BIN, None, "gcol"), P(BIN, None), P(BIN), P(BIN))
    return jax.shard_map(
        on_device,
        mesh=Mesh(devices, (*BIN, "gcol")),
        in_specs=placed,
        out_specs=P(BIN, None, None, "gcol"),
        check_vma=False,
    )
```

```python
import functools

import jax
import jax.numpy as jnp
from jax import lax
from jax.experimental import pallas as pl
from jax.experimental.pallas import tpu as pltpu
from jax.sharding import Mesh
from jax.sharding import PartitionSpec as P

NB = 256
GW = 128
LANES = 128
EXTRA = 8
WEIGHT_ROWS = 16
ROW = 8
BIN = ("y", "x", "core")
ORDER = ("x", "y", "core")
BF16 = jnp.bfloat16
F32 = jnp.float32
VMEM_BYTES = 24 * 1024 * 1024


def dot(a, b):
    return jnp.dot(a, b, preferred_element_type=F32)


def iota(shape, axis):
    return lax.broadcasted_iota(jnp.int32, shape, axis)


def call(kernel, out_shape, **options):
    return pl.pallas_call(
        kernel,
        out_shape=out_shape,
        compiler_params=pltpu.CompilerParams(vmem_limit_bytes=VMEM_BYTES),
        **options,
    )


def along_path(index):
    row, at = index // ROW, index % ROW
    return row * ROW + at + (row % 2) * (ROW - 1 - 2 * at)


def block_at(place):
    return place % ROW // 2 * ROW + place // ROW * 2 + place % 2


def slot_onehot(target, slots):
    return (iota((slots, target.shape[1]), 0) == target).astype(F32).astype(BF16)


def tile_rows(tile, part, capacity):
    at = (2 * tile + part) * capacity
    return slice(at, at + capacity)


def pack_rows_kernel(
    quarter_ref, owner_ref, offset_ref, frac_ref, rows_ref, target_ref, copy_ref, out_ref
):
    groups, depth, _ = out_ref.shape
    pairs = owner_ref.shape[1]
    tiles = rows_ref.shape[2] // LANES
    capacity = (depth - EXTRA) // (2 * tiles)
    for c in range(2):
        copy_ref[:, c * GW : (c + 1) * GW] = rows_ref[c, :, :GW]
    owner = owner_ref[...]
    named = (iota((groups, pairs), 0) == owner).astype(F32)
    before = (iota((pairs, pairs), 0) < iota((pairs, pairs), 1)).astype(F32).astype(BF16)
    rank = jnp.sum(dot(named.astype(BF16), before) * named, axis=0, keepdims=True)
    target = along_path(owner) * capacity + rank.astype(jnp.int32)
    target_ref[...] = target
    onehot = slot_onehot(target, groups * capacity)
    for c in range(2):
        packed = dot(onehot, rows_ref[c]).astype(BF16)
        for tile in range(tiles):
            part = packed[:, tile * LANES : (tile + 1) * LANES]
            out_ref[:, tile_rows(tile, c, capacity)] = part.reshape(groups, capacity, LANES)

    frac = frac_ref[...]
    place = iota((EXTRA, pairs), 0)
    weight = jnp.where(place == 0, (1.0 - frac).astype(BF16).astype(F32), 0.0)
    inside = owner * (NB // groups) + offset_ref[...] < NB - 1
    weight = jnp.where((place == 1) & inside, frac.astype(BF16).astype(F32), weight)
    weight = jnp.where(place == 2, offset_ref[...].astype(F32), weight)
    weight = lax.dot_general(
        weight.astype(BF16), onehot, (((1,), (1,)), ((), ())), preferred_element_type=F32
    )
    share = LANES // capacity
    quarter = quarter_ref[0]
    mine = iota((EXTRA, LANES), 1) // capacity == quarter
    for group in range(groups):
        tile = weight[:, group // share * LANES : (group // share + 1) * LANES]
        turn = (quarter + share - group % share) % share * capacity
        tile = jnp.where(mine, pltpu.roll(tile, turn, 1), 0.0)
        out_ref[group, depth - EXTRA :] = tile.astype(BF16)


def pack_heads_kernel(target_ref, head_ref, arrived_ref, table_ref, out_ref):
    groups, double, lanes = out_ref.shape
    capacity = double // 2
    onehot = slot_onehot(target_ref[...], groups * capacity)
    packed = dot(onehot, head_ref[...]).astype(BF16)
    for c in range(2):
        part = packed[:, c * lanes : (c + 1) * lanes]
        out_ref[:, c * capacity : (c + 1) * capacity] = part.reshape(groups, capacity, lanes)


def prepare_kernel(own_bins, got_ref, got_head_ref, head_ref, weight_ref, rows_ref, upper_ref):
    groups, double, lanes = got_head_ref.shape
    capacity = double // 2
    slots = groups * capacity
    share = LANES // capacity
    extra = got_ref.shape[1] - EXTRA
    for c in range(2):
        for tile in range(rows_ref.shape[1] // LANES):
            part = got_ref[:, tile_rows(tile, c, capacity)].reshape(slots, LANES)
            for at in range(c, 3, 2):
                rows_ref[
                    at * slots : (at + 1) * slots, tile * LANES : (tile + 1) * LANES
                ] = part
        head = got_head_ref[:, c * capacity : (c + 1) * capacity].reshape(slots, lanes)
        head_ref[c * lanes : (c + 1) * lanes] = head.astype(F32).T.astype(BF16)
    for at in range(groups // share):
        tile = got_ref[share * at, extra:].astype(F32)
        for k in range(1, share):
            tile += got_ref[share * at + k, extra:].astype(F32)
        low, high, offset = (tile[n : n + 1] for n in range(3))
        place = iota((WEIGHT_ROWS, LANES), 0).astype(F32)
        weight = jnp.where(place == offset, low, 0.0) + jnp.where(place == offset + 1.0, high, 0.0)
        weight_ref[:, at * LANES : (at + 1) * LANES] = weight
    weight = weight_ref[own_bins : own_bins + 1]
    scaled = [
        (head_ref[c * GW : (c + 1) * GW].astype(F32) * weight).astype(BF16) for c in range(2)
    ]
    for c, part in enumerate(complex_dot(scaled, rows_ref)):
        upper_ref[c] = part.astype(BF16)


def complex_dot(left, rows_ref):
    slots = rows_ref.shape[0] // 3
    real = dot(jnp.concatenate(left, axis=1), rows_ref[: 2 * slots])
    imag = dot(jnp.concatenate([left[0], -left[1]], axis=1), rows_ref[slots:])
    return real, imag


def spectral_kernel(own_bins, head_ref, weight_ref, rows_ref, out_ref):
    chunk, per, bins, width = out_ref.shape
    window = chunk * per
    slots = weight_ref.shape[1]
    at = pl.program_id(0) * window
    scaled = []
    for c in range(2):
        head = head_ref[pl.ds(pl.multiple_of(c * GW + at, window), window)].astype(F32)
        part = (head[:, None, :] * weight_ref[:own_bins][None]).astype(BF16)
        scaled.append(part.reshape(window * own_bins, slots))
    result = [part.reshape(window, own_bins, width) for part in complex_dot(scaled, rows_ref)]
    result = jnp.concatenate(result, axis=1).reshape(chunk, per, bins, width)
    out_ref[...] = result.astype(BF16)


def carry_kernel(spectral_ref, upper_ref, out_ref):
    groups, per, bins, width = out_ref.shape
    place = iota((groups * per, bins, width), 1)
    added = jnp.zeros((groups * per, bins, width), F32)
    for c in range(2):
        upper = upper_ref[c].astype(F32).reshape(groups * per, 1, width)
        added = jnp.where(place == c * (bins // 2), upper, added)
    values = spectral_ref[...].reshape(groups * per, bins, width) + added.astype(BF16)
    out_ref[...] = values.reshape(groups, per, bins, width)


def table_kernel(own_bins, out_ref):
    shape = (out_ref.shape[0] // 2, out_ref.shape[1])
    row = iota(shape, 0)
    column = iota(shape, 1)
    group = 2 * own_bins
    frequency = (block_at(row // group) * own_bins + row % own_bins).astype(F32)
    bin_at = (along_path(column // group) * own_bins + column % own_bins).astype(F32)
    row_imag = row // own_bins % 2 == 1
    column_imag = column // own_bins % 2 == 1
    difference = frequency - bin_at
    second = frequency + bin_at + 1.0
    first_scale = 1.0 / (difference * difference + 1.0)
    second_scale = 1.0 / (second * second + 1.0)
    real_part = difference * first_scale - second * second_scale
    imag_part = second_scale - first_scale
    crossed = jnp.where(row_imag, imag_part, -imag_part)
    table = jnp.where(row_imag == column_imag, real_part, crossed)
    high = table.astype(BF16)
    out_ref[: shape[0]] = high
    out_ref[shape[0] :] = (table - high.astype(F32)).astype(BF16)


def hilbert_kernel(table_ref, in_ref, out_ref):
    groups, per, bins, width = out_ref.shape
    for g in range(per):
        values = in_ref[:, g].reshape(groups * bins, width)
        result = dot(table_ref[...], values)
        result = result[: groups * bins] + result[groups * bins :]
        out_ref[:, g] = result.astype(BF16).reshape(groups, bins, width)


def final_kernel(in_ref, out_ref, wide):
    groups, per, depth, lanes = in_ref.shape
    for k in range(lanes // LANES):
        at = slice(k * LANES, (k + 1) * LANES)
        wide[k] = in_ref[:, :, :, at].astype(F32).reshape(groups * per * depth, LANES)
        for c in range(2):
            for step in range(depth // 2):
                out_ref[step, c, :, at] = wide[
                    k, pl.ds(c * (depth // 2) + step, groups * per, stride=depth), :
                ]


def from_first(block, axis):
    place = lax.axis_index(axis)
    ahead = lax.ppermute(block, axis, [(0, 3)])
    behind = lax.ppermute(block, axis, [(0, 5)])
    block = jnp.where(place == 3, ahead, jnp.where(place == 5, behind, block))
    ahead = lax.ppermute(block, axis, [(0, 1), (3, 4), (5, 6)])
    behind = lax.ppermute(block, axis, [(0, 7), (3, 2)])
    use_ahead = (place == 1) | (place == 4) | (place == 6)
    use_behind = (place == 7) | (place == 2)
    return jnp.where(use_ahead, ahead, jnp.where(use_behind, behind, block))


def exchange(block):
    return lax.all_to_all(block, ORDER, split_axis=0, concat_axis=0, tiled=True)


def on_device(pair_rows, pair_owner, pair_offset, pair_frac):
    groups = lax.axis_size(BIN)
    pairs, _, columns = pair_rows.shape
    capacity = 2 * pairs // groups
    slots = groups * capacity
    own_bins = NB // groups
    per = GW // groups
    blocks = 1
    shape = jax.ShapeDtypeStruct
    scalar = pl.BlockSpec(memory_space=pltpu.SMEM)
    here = pl.BlockSpec(memory_space=pltpu.VMEM)

    quarter = lax.axis_index(ORDER) % (LANES // capacity)
    by_part = jnp.swapaxes(pair_rows, 0, 1)
    target, head, packed = call(
        pack_rows_kernel,
        [
            shape((1, pairs), jnp.int32),
            shape((pairs, 2 * GW), BF16),
            shape((groups, 2 * capacity * columns // LANES + EXTRA, LANES), BF16),
        ],
        in_specs=[scalar] + [here] * 4,
    )(
        quarter.reshape(1),
        pair_owner.reshape(1, pairs),
        pair_offset.reshape(1, pairs),
        pair_frac.reshape(1, pairs),
        by_part,
    )
    got = exchange(packed)
    head = from_first(head, "gcol")
    table = call(
        functools.partial(table_kernel, own_bins), shape((4 * NB, 2 * NB), BF16)
    )()
    got_head = exchange(
        call(
            pack_heads_kernel,
            shape((groups, 2 * capacity, GW), BF16),
            in_specs=[here] * 2 + [pl.BlockSpec(memory_space=pl.ANY)] * 2,
        )(target, head, got, table)
    )

    whole = lambda *dims: pl.BlockSpec(dims, lambda i: (0,) * len(dims))
    head, weight, rows, upper = call(
        functools.partial(prepare_kernel, own_bins),
        [
            shape((2 * GW, slots), BF16),
            shape((WEIGHT_ROWS, slots), F32),
            shape((3 * slots, columns), BF16),
            shape((2, GW, columns), BF16),
        ],
    )(got, got_head)
    path = [block_at(along_path(i)) for i in range(groups)]
    upper = lax.ppermute(upper, BIN, list(zip(path, path[1:] + path[:1])))
    spectral = call(
        functools.partial(spectral_kernel, own_bins),
        shape((groups, per, 2 * own_bins, columns), BF16),
        grid=(blocks,),
        in_specs=[whole(2 * GW, slots), whole(WEIGHT_ROWS, slots), whole(3 * slots, columns)],
        out_specs=pl.BlockSpec(
            (groups // blocks, per, 2 * own_bins, columns), lambda i: (i, 0, 0, 0)
        ),
    )(head, weight, rows)
    spectral = call(
        carry_kernel, shape(spectral.shape, BF16), input_output_aliases={0: 0}
    )(spectral, upper)
    chi = call(hilbert_kernel, shape(spectral.shape, BF16))(table, exchange(spectral))
    return call(
        final_kernel,
        shape((own_bins, 2, GW, columns), F32),
        grid=(2,),
        in_specs=[
            pl.BlockSpec((groups, per, 2 * own_bins, columns // 2), lambda i: (0, 0, 0, i))
        ],
        out_specs=pl.BlockSpec((own_bins, 2, GW, columns // 2), lambda i: (0, 0, 0, i)),
        scratch_shapes=[pltpu.VMEM((columns // LANES // 2, GW * 2 * own_bins, LANES), F32)],
    )(exchange(chi))


def solution(mesh):
    bins, columns = mesh.devices.shape
    devices = mesh.devices.reshape(bins // ROW, ROW // 2, 2, columns)
    placed = (P(BIN, None, "gcol"), P(BIN, None), P(BIN), P(BIN))
    return jax.shard_map(
        on_device,
        mesh=Mesh(devices, (*BIN, "gcol")),
        in_specs=placed,
        out_specs=P(BIN, None, None, "gcol"),
        check_vma=False,
    )
```
